128 devices in a mesh: gx: 4 (over x), gy: 8 (over z, core), gz: 4 (over y).
Axes of the slice: x: 4, y: 4, z: 4, core: 2. Of those that a mesh axis runs over, the one named last changes fastest.
Arguments:
- right_side: float32 [64, 256, 1024], P('gx', 'gy', 'gz'), may hold values from -6 to 6
- conductivity: float32 [64, 256, 1024], P('gx', 'gy', 'gz'), may hold values from 0.2 to 5
- absorption: float32 [64, 256, 1024], P('gx', 'gy', 'gz'), may hold values from 0.01 to 0.3
Outputs:
- solution_field: float32 [64, 256, 1024], P('gx', 'gy', 'gz')
- residual: float32 [64, 256, 1024], P('gx', 'gy', 'gz')
The draws below stay inside these ranges and needn't reach their ends.
All inputs are finite; a program needn't handle non-finite values.
Results may differ from the reference program's by a relative error of at most 0.0003.
Values sent between devices are 32-bit elements; how exact they have to be, the bound alone decides.
A program may use at most 128 MiB of HBM per device.

```python
import math
import jax
import jax.numpy as jnp

SWEEPS = 2
COARSE_SWEEPS = 6
NX = 64
NY = 256
NZ = 1024


def block_levels(own_key, shape, shards, low, top_value):
    factor_of = 1.0
    for dim, blocks in shards:
        heights = jax.random.uniform(jax.random.fold_in(jax.random.fold_in(own_key, 6), dim), (blocks,), jnp.float32, low / len(shards), top_value / len(shards))
        factor_of = factor_of * jnp.repeat(jnp.exp(heights), shape[dim] // blocks).reshape((-1,) + (1,) * (len(shape) - 1 - dim))
    return factor_of


def normal_values(key, extent, deviation, bound, cuts=(), dtype=jnp.bfloat16):
    gain = block_levels(key, extent, cuts, -0.22, 0.18) if cuts else 1.0
    entries = jax.random.normal(key, extent, jnp.float32) * deviation * gain
    return jnp.minimum(jnp.maximum(entries, -bound), bound).astype(dtype)


def setup_inputs(seed: int = 0) -> dict:
    arg_keys = jax.random.split(jax.random.key(seed), 4)
    return {
        "right_side": normal_values(arg_keys[0], (NX, NY, NZ), 1.0, 6.0, ((0, 4), (1, 8), (2, 4)), jnp.float32),
        "conductivity": jnp.clip(jnp.exp(math.log(5.0) - 3.218876 * jax.random.uniform(arg_keys[1], (NX, NY, NZ), jnp.float32) ** block_levels(arg_keys[1], (NX, NY, NZ), ((0, 4), (1, 8), (2, 4)), -0.2, 0.2)), 0.2, 5.0),
        "absorption": jnp.clip(jnp.exp(math.log(0.3) - 3.4011974 * jax.random.uniform(arg_keys[2], (NX, NY, NZ), jnp.float32) ** block_levels(arg_keys[2], (NX, NY, NZ), ((0, 4), (1, 8), (2, 4)), -0.2, 0.2)), 0.01, 0.3),
    }


EIGEN_LOW = 0.25
EIGEN_HIGH = 2.0


def chebyshev_weights(count):
    middle = 0.5 * (EIGEN_HIGH + EIGEN_LOW)
    radius = 0.5 * (EIGEN_HIGH - EIGEN_LOW)
    return [1.0 / (middle + radius * math.cos(math.pi * (2 * step + 1) / (2 * count))) for step in range(count)]


def neighbor_list(padded):
    return [padded[2:, 1:-1, 1:-1], padded[:-2, 1:-1, 1:-1],
            padded[1:-1, 2:, 1:-1], padded[1:-1, :-2, 1:-1],
            padded[1:-1, 1:-1, 2:], padded[1:-1, 1:-1, :-2]]


def face_values(cond_field, padded):
    return [jnp.where(other > 0.0, 0.5 * (cond_field + other), cond_field) for other in neighbor_list(padded)]


def operate(field, padded, level):
    faces, absb_field, inverse, scale = level
    total = jnp.zeros_like(field)
    for face, other in zip(faces, neighbor_list(padded)):
        total = total + face * (field - other)
    return absb_field * field + scale * total


def build_level(cond_field, absb_field, scale, padder):
    faces = face_values(cond_field, padder(cond_field))
    total = jnp.zeros_like(cond_field)
    for face in faces:
        total = total + face
    return (faces, absb_field, 1.0 / (absb_field + scale * total), scale)


def smooth(guess, source, level, padder, weights):
    for weight in weights:
        if guess is None:
            remain = source
            guess = jnp.zeros_like(source)
        else:
            remain = source - operate(guess, padder(guess), level)
        guess = guess + weight * level[2] * remain
    return guess


def coarsen(field):
    sizex, sizey, sizez = field.shape
    return field.reshape(sizex // 2, 2, sizey // 2, 2, sizez // 2, 2).mean(axis=(1, 3, 5))


def refine(field):
    return jnp.repeat(jnp.repeat(jnp.repeat(field, 2, axis=0), 2, axis=1), 2, axis=2)


def pad_zero(field):
    return jnp.pad(field, 1)


def reference(right_side, conductivity, absorption):
    levels = []
    cond_field, absb_field = conductivity, absorption
    for depth in range(4):
        if depth > 0:
            cond_field = coarsen(cond_field)
            absb_field = coarsen(absb_field)
        levels.append(build_level(cond_field, absb_field, 0.25 ** depth, pad_zero))
    fine_weights = chebyshev_weights(SWEEPS)
    sources = [right_side]
    guesses = []
    for depth in range(3):
        guess = smooth(None, sources[depth], levels[depth], pad_zero, fine_weights)
        guesses.append(guess)
        remain = sources[depth] - operate(guess, pad_zero(guess), levels[depth])
        sources.append(coarsen(remain))
    correction = smooth(None, sources[3], levels[3], pad_zero, chebyshev_weights(COARSE_SWEEPS))
    for depth in (2, 1, 0):
        guess = guesses[depth] + refine(correction)
        correction = smooth(guess, sources[depth], levels[depth], pad_zero, fine_weights)
    residual = right_side - operate(correction, pad_zero(correction), levels[0])
    return correction, residual
```

```python
import functools
import math

import jax
import jax.numpy as jnp
from jax import lax
from jax.experimental import pallas as pl
from jax.experimental.pallas import tpu as pltpu
from jax.sharding import PartitionSpec as P

MESH = pl.DeviceIdType.MESH
AXES = ("gx", "gy", "gz")
EIGEN_LOW = 0.25
EIGEN_HIGH = 2.0
F32 = jnp.float32


def chebyshev_weights(count):
    middle = 0.5 * (EIGEN_HIGH + EIGEN_LOW)
    radius = 0.5 * (EIGEN_HIGH - EIGEN_LOW)
    return [
        1.0 / (middle + radius * math.cos(math.pi * (2 * step + 1) / (2 * count)))
        for step in range(count)
    ]


W = chebyshev_weights(2)
W6 = chebyshev_weights(6)


class Level:
    def __init__(self, scale, own, planes, first, rows, lanes, reach):
        self.scale = scale
        self.nx, self.ny, self.nz = own
        self.planes, self.first = planes, first
        self.rows, self.lanes = rows, lanes
        self.hy, self.hz = reach

    @property
    def shape(self):
        return (self.planes, self.rows, self.lanes)


L0 = Level(1.0, (16, 32, 256), 26, 5, 48, 384, (5, 8))
L1 = Level(0.25, (8, 16, 128), 22, 7, 32, 256, (7, 8))
L2 = Level(0.25**2, (4, 8, 64), 20, 2, 48, 128, (16, 32))
L3 = Level(0.25**3, (2, 4, 32), 10, 1, 24, 128, (8, 16))


def partner(offset, sizes):
    place = []
    for axis, step, size in zip(AXES, offset, sizes):
        index = lax.axis_index(axis)
        place.append(index if step == 0 else lax.rem(index + (step + size), size))
    return tuple(place)


def up(value, axis):
    return pltpu.roll(value, value.shape[axis] - 1, axis)


def down(value, axis):
    return pltpu.roll(value, 1, axis)


def iota(shape, axis):
    return lax.broadcasted_iota(jnp.int32, shape, axis)


def make_mask(lev, sizes, mask_ref, miss_ref):
    shape = (lev.rows, lev.lanes)
    gy, gz = lax.axis_index("gy"), lax.axis_index("gz")
    row, lane = iota(shape, 0), iota(shape, 1)
    y = jnp.where(row < lev.ny + lev.hy, row, row - lev.rows)
    z = jnp.where(lane < lev.nz + lev.hz, lane, lane - lev.lanes)
    yy, zz = y + gy * lev.ny, z + gz * lev.nz
    ymax, zmax = lev.ny * sizes[1], lev.nz * sizes[2]
    good = (y >= -lev.hy) & (z >= -lev.hz) & (yy >= 0) & (yy < ymax) & (zz >= 0) & (zz < zmax)
    mask_ref[...] = jnp.where(good, 1.0, 0.0)
    miss = jnp.where(yy == 0, 1.0, 0.0) + jnp.where(yy == ymax - 1, 1.0, 0.0)
    miss_ref[...] = miss + jnp.where(zz == 0, 1.0, 0.0) + jnp.where(zz == zmax - 1, 1.0, 0.0)


def build(lev, base, xmax, lo, hi, e, c_ref, mask_ref, miss_ref, fx, fy, fz, inv, diag, src, v, weight):
    scale = lev.scale

    def masked(p):
        x = p + base
        bar = jnp.where((x >= 0) & (x < xmax), 0.5, 2.0)
        keep = mask_ref[...] > bar
        return keep, jnp.where(keep, e[0, p], 0.0)

    def face(a, b):
        return jnp.where(jnp.minimum(a, b) > 0.0, (0.5 * scale) * (a + b), 0.0)

    before = masked(lo - 1)[1]
    c_ref[0] = before
    keep, cur = masked(lo)
    c_ref[1] = cur
    fx[lo - 1] = face(before, cur)

    def body(p, carry):
        cur = c_ref[1]
        keep, after = masked(p + 1)
        x = p + base
        mine = mask_ref[...] > jnp.where((x >= 0) & (x < xmax), 0.5, 2.0)
        fxp = face(cur, after)
        fx[p] = fxp
        fyp = face(cur, up(cur, 0))
        fy[p] = fyp
        fzp = face(cur, up(cur, 1))
        fz[p] = fzp
        edge = jnp.where(x == 0, 1.0, 0.0) + jnp.where(x == xmax - 1, 1.0, 0.0)
        total = fx[p - 1] + fxp + fyp + down(fyp, 0) + fzp + down(fzp, 1)
        total = total + (scale * cur) * (miss_ref[...] + edge)
        d = e[1, p] + total
        diag[p] = jnp.where(mine, d, 0.0)
        i = jnp.where(mine, 1.0 / d, 0.0)
        inv[p] = i
        if weight is not None:
            s = jnp.where(mine, e[2, p], 0.0)
            src[p] = s
            v[p] = weight * i * s
        c_ref[1] = after
        return carry

    lax.fori_loop(lo, hi, body, 0)


def first_sweep(lev, base, xmax, lo, hi, e, mask_ref, inv, src, v, weight):
    def body(p, carry):
        x = p + base
        mine = mask_ref[...] > jnp.where((x >= 0) & (x < xmax), 0.5, 2.0)
        s = jnp.where(mine, e[2, p], 0.0)
        src[p] = s
        v[p] = weight * inv[p] * s
        return carry

    lax.fori_loop(lo, hi, body, 0)


def flow(p, v, fx, fy, fz):
    cur = v[p]
    fyp, fzp = fy[p], fz[p]
    total = fx[p] * v[p + 1] + fx[p - 1] * v[p - 1]
    total = total + (fyp * up(cur, 0) + down(fyp * cur, 0))
    return cur, total + (fzp * up(cur, 1) + down(fzp * cur, 1))


def sweep(lo, hi, src, fx, fy, fz, inv, v, out, weight):
    def body(p, carry):
        cur, total = flow(p, v, fx, fy, fz)
        out[p] = (1.0 - weight) * cur + (weight * inv[p]) * (src[p] + total)
        return carry

    lax.fori_loop(lo, hi, body, 0)


def remainder(p, src, fx, fy, fz, diag, v):
    cur, total = flow(p, v, fx, fy, fz)
    return (src[p] - diag[p] * cur) + total


def pool_matrix(fine, coarse):
    shape = (fine.lanes, coarse.lanes)
    f, c = iota(shape, 0), iota(shape, 1)
    zf = jnp.where(f < fine.nz + fine.hz, f, f - fine.lanes)
    zc = jnp.where(c < coarse.nz + coarse.hz, c, c - coarse.lanes)
    hit = (zf >= 2 * zc) & (zf < 2 * zc + 2) & (zc >= -coarse.hz)
    return jnp.where(hit, 0.125, 0.0)


def spread_matrix(coarse, fine):
    shape = (coarse.lanes, fine.lanes)
    c, f = iota(shape, 0), iota(shape, 1)
    zf = jnp.where(f < fine.nz + fine.hz, f, f - fine.lanes)
    zc = jnp.where(c < coarse.nz + coarse.hz, c, c - coarse.lanes)
    hit = (zf >= 2 * zc) & (zf < 2 * zc + 2) & (zf >= -fine.hz)
    return jnp.where(hit, 1.0, 0.0)


def dot(a, b):
    return jnp.dot(a, b, preferred_element_type=F32, precision=lax.Precision.HIGHEST)


def pair_rows(value, tmp):
    rows, lanes = value.shape
    parts = []
    for k in range(lanes // 128):
        tmp[k, pl.ds(0, rows)] = value[:, 128 * k : 128 * (k + 1)]
    for k in range(lanes // 128):
        even = tmp[k, pl.ds(0, rows // 2, stride=2)]
        odd = tmp[k, pl.ds(1, rows // 2, stride=2)]
        parts.append(even + odd)
    return parts[0] if len(parts) == 1 else jnp.concatenate(parts, axis=1)


def coarsen(pairs, get, matrix, tmp, put):
    def body(q, carry):
        rows = pair_rows(get(2 * q) + get(2 * q + 1), tmp)
        put(q, dot(rows, matrix[...]))
        return carry

    lax.fori_loop(0, pairs, body, 0)


def pack(lev, a_count, a_first, e, zs):
    shape = (lev.ny, 128)
    group = lax.shift_right_logical(iota(shape, 1), 3)
    for a in range(a_count):

        def body(x, carry):
            low, high = carry
            p = lev.first + x
            lows = pltpu.roll(e[a_first + a, p, pl.ds(0, lev.ny), pl.ds(0, 128)], 8 * x, 1)
            highs = e[a_first + a, p, pl.ds(0, lev.ny), pl.ds(lev.nz - 128, 128)]
            highs = pltpu.roll(highs, lax.rem(8 * x + 8, 128), 1)
            here = group == x
            return jnp.where(here, lows, low), jnp.where(here, highs, high)

        zero = jnp.zeros(shape, F32)
        low, high = lax.fori_loop(0, lev.nx, body, (zero, zero))
        zs[0, a] = low
        zs[1, a] = high


def unpack(lev, a_count, a_first, e, zr):
    lane = iota((lev.rows, 128), 1)
    spans = ((0, 0, lev.first), (1, lev.first, lev.nx), (2, lev.first + lev.nx, lev.first))
    for slot, start, count in spans:
        offset = lev.nx - lev.first if slot == 0 else 0

        def body(k, carry):
            x = k + offset
            for a in range(a_count):
                low = pltpu.roll(zr[0, slot, a], 120 - 8 * x, 1)
                high = pltpu.roll(zr[1, slot, a], lax.rem(128 - 8 * x, 128), 1)
                e[a_first + a, start + k, :, pl.ds(lev.nz, 128)] = jnp.where(lane < 64, high, low)
            return carry

        lax.fori_loop(0, count, body, 0)


def halo_messages(lev, a_first, a_count, widths, e, zs, zr):
    first, nx, ny, rows, hy = lev.first, lev.nx, lev.ny, lev.rows, lev.hy

    def planes(dx, w):
        if dx == 0:
            return pl.ds(first, nx), pl.ds(first, nx)
        if dx > 0:
            return pl.ds(first + nx - w, w), pl.ds(first - w, w)
        return pl.ds(first, w), pl.ds(first + nx, w)

    def lines(dy):
        if dy == 0:
            return pl.ds(0, ny), pl.ds(0, ny)
        if dy > 0:
            return pl.ds(ny - hy, hy), pl.ds(rows - hy, hy)
        return pl.ds(0, hy), pl.ds(ny, hy)

    found = []
    for dz in (0, -1, 1):
        for dx in (1, -1, 0):
            for dy in (0, 1, -1):
                if dx == dy == dz == 0:
                    continue
                ys, yd = lines(dy)
                if dz == 0:
                    groups = [(a_first, a_count, max(widths))]
                    if dy == 0 and len(widths) > 1:
                        groups = []
                        a = a_first
                        for w, n in ((widths[0], 1), (widths[1], a_count - 1)):
                            groups.append((a, n, w))
                            a += n
                    for a, n, w in groups:
                        xs, xd = planes(dx, w)
                        found.append(
                            (
                                e.at[pl.ds(a, n), xs, ys, pl.ds(0, lev.nz)],
                                e.at[pl.ds(a, n), xd, yd, pl.ds(0, lev.nz)],
                                (dx, dy, dz),
                            )
                        )
                else:
                    side = 1 if dz > 0 else 0
                    slot = 1 - dx
                    found.append(
                        (zs.at[side, :, ys], zr.at[1 - side, slot, :, yd], (dx, dy, dz))
                    )
    return found


GATHER = [
    (dx, 0, dz) for dx in (1, 3, 2, 0) for dz in (0, 1, -1) if (dx, dz) != (0, 0)
]
NEAR = [
    (dx, dy, dz)
    for dx in (-1, 0, 1)
    for dy in (-1, 0, 1)
    for dz in (-1, 0, 1)
    if (dx, dy, dz) != (0, 0, 0)
]
FAR = [(2, 0, 0), (2, 0, 1), (2, 0, -1), (0, 2, 0), (0, -2, 0)]
MESSAGES = 28 + 26 + 26 + 15 + 15


def kernel(
    sizes, rhs, cond, absb, sol, res,
    e0, fx0, fy0, fz0, inv0, diag0, src0, v0, u0, mask0, miss0, zs0, zr0,
    e1, fx1, fy1, fz1, inv1, diag1, src1, v1, u1, mask1, miss1, zs1, zr1, zt1, zu1,
    e2, fx2, fy2, fz2, inv2, diag2, src2, v2, u2, mask2, miss2, own2, gat2,
    e3, fx3, fy3, fz3, inv3, diag3, src3, v3, u3, mask3, miss3,
    p01, p12, p23, s32, s21, s10, c0, c1, c2, c3, tmp, rout, send, recv, local,
):
    gx, gy, gz = (lax.axis_index(axis) for axis in AXES)
    own0 = (pl.ds(L0.first, L0.nx), pl.ds(0, L0.ny), pl.ds(0, L0.nz))
    loads = [
        pltpu.make_async_copy(source, e0.at[(a,) + own0], local.at[a])
        for a, source in enumerate((cond, absb, rhs))
    ]
    for copy in loads:
        copy.start()

    barrier = pltpu.get_barrier_semaphore()
    for offset in NEAR + FAR:
        pl.semaphore_signal(
            barrier, inc=1, device_id=partner(offset, sizes), device_id_type=MESH
        )
    for lev, mask, miss in ((L0, mask0, miss0), (L1, mask1, miss1), (L2, mask2, miss2), (L3, mask3, miss3)):
        make_mask(lev, sizes, mask, miss)
    p01[...] = pool_matrix(L0, L1)[:256, :128]
    p12[...] = pool_matrix(L1, L2)[:128]
    p23[...] = pool_matrix(L2, L3)
    s32[...] = spread_matrix(L3, L2)
    s21[...] = spread_matrix(L2, L1)
    s10[...] = spread_matrix(L1, L0)
    for p in (0, 1, 18, 19):
        for ref in (e2.at[0], v2, u2):
            ref[p] = jnp.zeros((L2.rows, L2.lanes), F32)
    for p in (0, 9):
        for ref in (e3.at[0], v3, u3):
            ref[p] = jnp.zeros((L3.rows, L3.lanes), F32)
    for copy in loads:
        copy.wait()
    pack(L0, 3, 0, e0, zs0)
    pl.semaphore_wait(barrier, len(NEAR + FAR))

    started = []

    def post(messages):
        copies = []
        for source, target, offset in messages:
            k = len(started)
            copy = pltpu.make_async_remote_copy(
                src_ref=source,
                dst_ref=target,
                send_sem=send.at[k],
                recv_sem=recv.at[k],
                device_id=partner(offset, sizes),
                device_id_type=MESH,
            )
            copy.start()
            started.append(copy)
            copies.append(copy)
        return copies

    def arrive(copies):
        for copy in copies:
            copy.wait_recv()

    def gather_a(a, n):
        x = pl.ds(L2.first + L2.nx * gx, L2.nx)
        return [
            (own2.at[pl.ds(a, n)], gat2.at[1 - offset[2], pl.ds(a, n), x], offset)
            for offset in GATHER
        ]

    def gather_b(a, n):
        x = pl.ds(L2.first, 16)
        mine = e2.at[pl.ds(a, n), x, pl.ds(0, 8)]
        return [
            (mine, e2.at[pl.ds(a, n), x, pl.ds(row, 8)], (0, dy, 0))
            for dy, row in ((1, 40), (-1, 8), (2, 32), (-2, 16))
        ]

    def keep_own(a):
        gat2[1, a, pl.ds(L2.first + L2.nx * gx, L2.nx)] = own2[a]

    def combine(a):
        lane = iota((L2.ny, 128), 1)

        def body(p, carry):
            far = pltpu.roll(jnp.where(lane < 32, gat2[2, a, p], gat2[0, a, p]), 64, 1)
            e2[a, p, pl.ds(0, 8)] = jnp.where(lane < 64, gat2[1, a, p], far)
            return carry

        lax.fori_loop(L2.first, L2.first + 16, body, 0)

    round_1 = post(halo_messages(L0, 0, 3, (5, 4), e0, zs0, zr0))

    for a in range(2):

        def put1(q, plane, a=a):
            e1[a, L1.first + q, pl.ds(0, 16), pl.ds(0, 128)] = plane

        coarsen(8, lambda p, a=a: e0[a, L0.first + p, pl.ds(0, 32), pl.ds(0, 256)], p01, tmp, put1)
    pack(L1, 2, 0, e1, zs1)
    round_c1 = post(halo_messages(L1, 0, 2, (7,), e1, zs1, zr1))
    for a in range(2):

        def put2(q, plane, a=a):
            own2[a, q] = plane

        coarsen(4, lambda p, a=a: e1[a, L1.first + p, pl.ds(0, 16), pl.ds(0, 128)], p12, tmp, put2)
        keep_own(a)
    round_c2 = post(gather_a(0, 2))

    base0 = L0.nx * gx - L0.first
    arrive(round_1)
    unpack(L0, 3, 0, e0, zr0)
    build(L0, base0, 64, 1, 25, e0, c0, mask0, miss0, fx0, fy0, fz0, inv0, diag0, src0, v0, W[0])
    sweep(2, 24, src0, fx0, fy0, fz0, inv0, v0, u0, W[1])

    def res0(p):
        return remainder(L0.first + p, src0, fx0, fy0, fz0, diag0, u0)[:32, :256]

    def put_s1(q, plane):
        e1[2, L1.first + q, pl.ds(0, 16), pl.ds(0, 128)] = plane

    coarsen(8, res0, p01, tmp, put_s1)
    pack(L1, 1, 2, e1, zt1)
    round_2 = post(halo_messages(L1, 2, 1, (6,), e1, zt1, zu1))

    base1 = L1.nx * gx - L1.first
    arrive(round_c1)
    unpack(L1, 2, 0, e1, zr1)
    build(L1, base1, 32, 1, 21, e1, c1, mask1, miss1, fx1, fy1, fz1, inv1, diag1, src1, v1, None)
    arrive(round_c2)
    for a in range(2):
        combine(a)
    round_d2 = post(gather_b(0, 2))
    arrive(round_2)
    unpack(L1, 1, 2, e1, zu1)
    first_sweep(L1, base1, 32, 1, 21, e1, mask1, inv1, src1, v1, W[0])
    sweep(2, 20, src1, fx1, fy1, fz1, inv1, v1, u1, W[1])

    def res1(p):
        return remainder(L1.first + p, src1, fx1, fy1, fz1, diag1, u1)[:16, :128]

    def put_s2(q, plane):
        own2[2, q] = plane

    coarsen(4, res1, p12, tmp, put_s2)
    keep_own(2)
    round_3 = post(gather_a(2, 1))

    arrive(round_d2)
    build(L2, -L2.first, 16, 2, 18, e2, c2, mask2, miss2, fx2, fy2, fz2, inv2, diag2, src2, v2, None)
    for a in range(2):

        def put3(q, plane, a=a):
            e3[a, L3.first + q] = plane

        coarsen(8, lambda p, a=a: e2[a, L2.first + p], p23, tmp, put3)
    build(L3, -L3.first, 8, 1, 9, e3, c3, mask3, miss3, fx3, fy3, fz3, inv3, diag3, src3, v3, None)

    arrive(round_3)
    combine(2)
    round_4 = post(gather_b(2, 1))
    arrive(round_4)

    first_sweep(L2, -L2.first, 16, 2, 18, e2, mask2, inv2, src2, v2, W[0])
    sweep(2, 18, src2, fx2, fy2, fz2, inv2, v2, u2, W[1])

    def put_s3(q, plane):
        e3[2, L3.first + q] = plane

    coarsen(8, lambda p: remainder(L2.first + p, src2, fx2, fy2, fz2, diag2, u2), p23, tmp, put_s3)
    first_sweep(L3, -L3.first, 8, 1, 9, e3, mask3, inv3, src3, v3, W6[0])
    here, there = v3, u3
    for weight in W6[1:]:
        sweep(1, 9, src3, fx3, fy3, fz3, inv3, here, there, weight)
        here, there = there, here

    def refine(count, get, matrix, rows, wrap, put):
        def body(q, carry):
            plane = get(q)
            wide = dot(plane, matrix[...])
            for k in range(wide.shape[1] // 128):
                part = wide[:, 128 * k : 128 * (k + 1)]
                for odd in (0, 1):
                    tmp[k, pl.ds(odd, rows, stride=2)] = part[:rows]
                    if wrap:
                        tmp[k, pl.ds(2 * (rows - wrap) + odd, wrap, stride=2)] = part[part.shape[0] - wrap :]
            done = [tmp[k, pl.ds(0, 2 * rows)] for k in range(wide.shape[1] // 128)]
            put(q, done[0] if len(done) == 1 else jnp.concatenate(done, axis=1))
            return carry

        lax.fori_loop(0, count, body, 0)

    def add2(q, plane):
        for k in (0, 1):
            u2[L2.first + 2 * q + k] += plane

    refine(8, lambda q: here[L3.first + q], s32, 24, 0, add2)
    sweep(2, 18, src2, fx2, fy2, fz2, inv2, u2, v2, W[0])
    sweep(2, 18, src2, fx2, fy2, fz2, inv2, v2, u2, W[1])

    def add1(q, plane):
        for k in (0, 1):
            u1[L1.first - 4 + 2 * q + k] += plane

    refine(8, lambda q: u2[L2.nx * gx + q], s21, 16, 4, add1)
    sweep(4, 18, src1, fx1, fy1, fz1, inv1, u1, v1, W[0])
    sweep(5, 17, src1, fx1, fy1, fz1, inv1, v1, u1, W[1])

    def add0(q, plane):
        for k in (0, 1):
            u0[L0.first - 4 + 2 * q + k] += plane

    refine(12, lambda q: u1[L1.first - 2 + q], s10, 24, 4, add0)
    sweep(3, 23, src0, fx0, fy0, fz0, inv0, u0, v0, W[0])
    sweep(4, 22, src0, fx0, fy0, fz0, inv0, v0, u0, W[1])
    stores = [pltpu.make_async_copy(u0.at[own0], sol, local.at[3])]
    stores[0].start()

    def last(p, carry):
        rout[p] = remainder(L0.first + p, src0, fx0, fy0, fz0, diag0, u0)[:32, :256]
        return carry

    lax.fori_loop(0, 16, last, 0)
    stores.append(pltpu.make_async_copy(rout, res, local.at[4]))
    stores[1].start()
    for copy in started:
        copy.wait_send()
    for copy in stores:
        copy.wait()


def solution(mesh):
    sizes = tuple(mesh.shape[axis] for axis in AXES)

    def vmem(*shape):
        return pltpu.VMEM(shape, F32)

    def level(lev):
        return [vmem(3, *lev.shape)] + [vmem(*lev.shape)] * 8 + [vmem(lev.rows, lev.lanes)] * 2

    scratch = [
        *level(L0), vmem(2, 3, 32, 128), vmem(2, 3, 3, 48, 128),
        *level(L1), vmem(2, 2, 16, 128), vmem(2, 3, 2, 32, 128), vmem(2, 1, 16, 128), vmem(2, 3, 1, 32, 128),
        *level(L2), vmem(3, 4, 8, 128), vmem(3, 3, 20, 8, 128),
        *level(L3),
        vmem(256, 128), vmem(128, 128), vmem(128, 128), vmem(128, 128), vmem(128, 256), vmem(256, 384),
        vmem(2, 48, 384), vmem(2, 32, 256), vmem(2, 48, 128), vmem(2, 24, 128),
        vmem(3, 48, 128), vmem(16, 32, 256),
        pltpu.SemaphoreType.DMA((MESSAGES,)),
        pltpu.SemaphoreType.DMA((MESSAGES,)),
        pltpu.SemaphoreType.DMA((5,)),
    ]

    def cycle(right_side, conductivity, absorption):
        block = jax.ShapeDtypeStruct((16, 32, 256), F32)
        return pl.pallas_call(
            functools.partial(kernel, sizes),
            out_shape=(block, block),
            in_specs=[pl.BlockSpec(memory_space=pl.ANY)] * 3,
            out_specs=(pl.BlockSpec(memory_space=pl.ANY),) * 2,
            scratch_shapes=scratch,
            compiler_params=pltpu.CompilerParams(
                collective_id=0, has_side_effects=True, vmem_limit_bytes=56 * 2**20
            ),
        )(right_side, conductivity, absorption)

    placed = P(*AXES)
    return jax.shard_map(
        cycle, mesh=mesh, in_specs=(placed,) * 3, out_specs=(placed, placed), check_vma=False
    )
```

```python
import functools
import math

import jax
import jax.numpy as jnp
from jax import lax
from jax.experimental import pallas as pl
from jax.experimental.pallas import tpu as pltpu
from jax.sharding import PartitionSpec as P

MESH = pl.DeviceIdType.MESH
AXES = ("gx", "gy", "gz")
EIGEN_LOW = 0.25
EIGEN_HIGH = 2.0
F32 = jnp.float32


def chebyshev_weights(count):
    middle = 0.5 * (EIGEN_HIGH + EIGEN_LOW)
    radius = 0.5 * (EIGEN_HIGH - EIGEN_LOW)
    return [
        1.0 / (middle + radius * math.cos(math.pi * (2 * step + 1) / (2 * count)))
        for step in range(count)
    ]


W = chebyshev_weights(2)
W6 = chebyshev_weights(6)


class Level:
    def __init__(self, scale, own, planes, first, rows, lanes, reach):
        self.scale = scale
        self.nx, self.ny, self.nz = own
        self.planes, self.first = planes, first
        self.rows, self.lanes = rows, lanes
        self.hy, self.hz = reach

    @property
    def shape(self):
        return (self.planes, self.rows, self.lanes)


L0 = Level(1.0, (16, 32, 256), 26, 5, 48, 384, (5, 8))
L1 = Level(0.25, (8, 16, 128), 22, 7, 32, 256, (7, 8))
L2 = Level(0.25**2, (4, 8, 64), 20, 2, 48, 128, (16, 32))
L3 = Level(0.25**3, (2, 4, 32), 10, 1, 24, 128, (8, 16))


def partner(offset, sizes):
    place = []
    for axis, step, size in zip(AXES, offset, sizes):
        index = lax.axis_index(axis)
        place.append(index if step == 0 else lax.rem(index + (step + size), size))
    return tuple(place)


def up(value, axis):
    return pltpu.roll(value, value.shape[axis] - 1, axis)


def down(value, axis):
    return pltpu.roll(value, 1, axis)


def iota(shape, axis):
    return lax.broadcasted_iota(jnp.int32, shape, axis)


def make_mask(lev, sizes, mask_ref, miss_ref):
    shape = (lev.rows, lev.lanes)
    gy, gz = lax.axis_index("gy"), lax.axis_index("gz")
    row, lane = iota(shape, 0), iota(shape, 1)
    y = jnp.where(row < lev.ny + lev.hy, row, row - lev.rows)
    z = jnp.where(lane < lev.nz + lev.hz, lane, lane - lev.lanes)
    yy, zz = y + gy * lev.ny, z + gz * lev.nz
    ymax, zmax = lev.ny * sizes[1], lev.nz * sizes[2]
    good = (y >= -lev.hy) & (z >= -lev.hz) & (yy >= 0) & (yy < ymax) & (zz >= 0) & (zz < zmax)
    mask_ref[...] = jnp.where(good, 1.0, 0.0)
    miss = jnp.where(yy == 0, 1.0, 0.0) + jnp.where(yy == ymax - 1, 1.0, 0.0)
    miss_ref[...] = miss + jnp.where(zz == 0, 1.0, 0.0) + jnp.where(zz == zmax - 1, 1.0, 0.0)


def blocks(lo, hi, step, body):
    full = (hi - lo) // step

    def one(i, carry):
        body(lo + i * step, step)
        return carry

    if full == 1:
        body(lo, step)
    elif full:
        lax.fori_loop(0, full, one, 0)
    if (hi - lo) % step:
        body(lo + full * step, (hi - lo) % step)


def inside(p, base, xmax, mask_ref):
    x = p + base
    return mask_ref[...] > jnp.where((x >= 0) & (x < xmax), 0.5, 2.0)


def build(lev, base, xmax, lo, hi, step, e, mask_ref, miss_ref, fx, fy, fz, inv, diag, src, v, weight):
    scale = lev.scale

    def face(a, b):
        return jnp.where(jnp.minimum(a, b) > 0.0, (0.5 * scale) * (a + b), 0.0)

    def masked(p):
        return jnp.where(inside(p, base, xmax, mask_ref), e[0, p], 0.0)

    fx[lo - 1] = face(masked(lo - 1), masked(lo))

    def body(p0, n):
        cur = masked(p0)
        fxm = fx[p0 - 1]
        for k in range(n):
            p = p0 + k
            x = p + base
            after = masked(p + 1)
            fxp = face(cur, after)
            fx[p] = fxp
            fyp = face(cur, up(cur, 0))
            fy[p] = fyp
            fzp = face(cur, up(cur, 1))
            fz[p] = fzp
            edge = jnp.where(x == 0, 1.0, 0.0) + jnp.where(x == xmax - 1, 1.0, 0.0)
            total = (fxm + fxp) + (fyp + down(fyp, 0)) + (fzp + down(fzp, 1))
            total = total + (scale * cur) * (miss_ref[...] + edge)
            mine = inside(p, base, xmax, mask_ref)
            d = e[1, p] + total
            diag[p] = jnp.where(mine, d, 0.0)
            i = jnp.where(mine, 1.0 / d, 0.0)
            inv[p] = i
            if weight is not None:
                s = jnp.where(mine, e[2, p], 0.0)
                src[p] = s
                v[p] = weight * i * s
            cur, fxm = after, fxp

    blocks(lo, hi, step, body)


def first_sweep(lev, base, xmax, lo, hi, step, e, mask_ref, inv, src, v, weight):
    def body(p0, n):
        for k in range(n):
            p = p0 + k
            s = jnp.where(inside(p, base, xmax, mask_ref), e[2, p], 0.0)
            src[p] = s
            v[p] = weight * inv[p] * s

    blocks(lo, hi, step, body)


def flow(p, v, fx, fy, fz):
    cur = v[p]
    fyp, fzp = fy[p], fz[p]
    total = fx[p] * v[p + 1] + fx[p - 1] * v[p - 1]
    total = total + (fyp * up(cur, 0) + down(fyp * cur, 0))
    return cur, total + (fzp * up(cur, 1) + down(fzp * cur, 1))


def sweep(lo, hi, step, src, fx, fy, fz, inv, v, out, weight):
    def body(p0, n):
        for k in range(n):
            p = p0 + k
            cur, total = flow(p, v, fx, fy, fz)
            out[p] = (1.0 - weight) * cur + (weight * inv[p]) * (src[p] + total)

    blocks(lo, hi, step, body)


def remainder(p, src, fx, fy, fz, diag, v):
    cur, total = flow(p, v, fx, fy, fz)
    return (src[p] - diag[p] * cur) + total


def pool_matrix(fine, coarse):
    shape = (fine.lanes, coarse.lanes)
    f, c = iota(shape, 0), iota(shape, 1)
    zf = jnp.where(f < fine.nz + fine.hz, f, f - fine.lanes)
    zc = jnp.where(c < coarse.nz + coarse.hz, c, c - coarse.lanes)
    hit = (zf >= 2 * zc) & (zf < 2 * zc + 2) & (zc >= -coarse.hz)
    return jnp.where(hit, 0.125, 0.0)


def spread_matrix(coarse, fine):
    shape = (coarse.lanes, fine.lanes)
    c, f = iota(shape, 0), iota(shape, 1)
    zf = jnp.where(f < fine.nz + fine.hz, f, f - fine.lanes)
    zc = jnp.where(c < coarse.nz + coarse.hz, c, c - coarse.lanes)
    hit = (zf >= 2 * zc) & (zf < 2 * zc + 2) & (zf >= -fine.hz)
    return jnp.where(hit, 1.0, 0.0)


def dot(a, b):
    high = a.astype(jnp.bfloat16)
    low = (a - high.astype(F32)).astype(jnp.bfloat16)
    b = b.astype(jnp.bfloat16)
    return jnp.dot(high, b, preferred_element_type=F32) + jnp.dot(low, b, preferred_element_type=F32)


def stage(tmp, q, plane):
    rows, lanes = plane.shape
    for k in range(lanes // 128):
        tmp[q, k, pl.ds(0, rows)] = plane[:, 128 * k : 128 * (k + 1)]


def pool(tmp, count, rows, tiles, matrix):
    parts = []
    for k in range(tiles):
        lines = []
        for q in range(count):
            even = tmp[q, k, pl.ds(0, rows // 2, stride=2)]
            odd = tmp[q, k, pl.ds(1, rows // 2, stride=2)]
            lines.append(even + odd)
        parts.append(jnp.concatenate(lines, axis=0))
    both = parts[0] if tiles == 1 else jnp.concatenate(parts, axis=1)
    done = dot(both, matrix[...])
    return [done[q * (rows // 2) : (q + 1) * (rows // 2)] for q in range(count)]


def spread(planes, tmp, matrix, rows, wrap):
    size = planes[0].shape[0]
    wide = dot(jnp.concatenate(planes, axis=0), matrix[...])
    for q in range(len(planes)):
        for k in range(wide.shape[1] // 128):
            part = wide[q * size : (q + 1) * size, 128 * k : 128 * (k + 1)]
            for odd in (0, 1):
                tmp[q, k, pl.ds(odd, rows - wrap, stride=2)] = part[: rows - wrap]
                if wrap:
                    tmp[q, k, pl.ds(2 * (rows - wrap) + odd, wrap, stride=2)] = part[size - wrap :]


def staged(tmp, q, rows, tiles):
    parts = [tmp[q, k, pl.ds(0, rows)] for k in range(tiles)]
    return parts[0] if tiles == 1 else jnp.concatenate(parts, axis=1)


def pack(lev, a_count, a_first, e, zs):
    shape = (lev.ny, 128)
    group = lax.shift_right_logical(iota(shape, 1), 3)
    for a in range(a_count):
        low = high = jnp.zeros(shape, F32)
        for x in range(lev.nx):
            p = lev.first + x
            lows = e[a_first + a, p, pl.ds(0, lev.ny), pl.ds(0, 128)]
            highs = e[a_first + a, p, pl.ds(0, lev.ny), pl.ds(lev.nz - 128, 128)]
            if x:
                lows = pltpu.roll(lows, 8 * x, 1)
            if x < 15:
                highs = pltpu.roll(highs, 8 * x + 8, 1)
            low = jnp.where(group == x, lows, low)
            high = jnp.where(group == x, highs, high)
        zs[0, a] = low
        zs[1, a] = high


def pack_edges(lev, zs, zx):
    shape = (lev.ny, 128)
    lane = iota(shape, 1)
    width = 8 * lev.first
    for side in (0, 1):
        for xside in (0, 1):
            total = jnp.zeros(shape, F32)
            for a in range(3):
                shift = width * a - (0 if xside == 0 else 128 - width)
                part = zs[side, a]
                if shift % 128:
                    part = pltpu.roll(part, shift % 128, 1)
                total = jnp.where((lane >= width * a) & (lane < width * (a + 1)), part, total)
            zx[side, xside] = total


def unpack_own(lev, e, zr):
    lane = iota((lev.rows, 128), 1)

    def body(x0, n):
        for k in range(n):
            x = x0 + k
            for a in range(3):
                low = pltpu.roll(zr[0, a], 120 - 8 * x, 1)
                high = pltpu.roll(zr[1, a], lax.rem(128 - 8 * x, 128), 1)
                e[a, lev.first + x, :, pl.ds(lev.nz, 128)] = jnp.where(lane < 64, high, low)

    blocks(0, lev.nx, 4, body)


def unpack_edges(lev, e, zq):
    lane = iota((lev.rows, 128), 1)
    for slot in (0, 1):
        for a in range(3):
            for k in range(lev.first):
                x = a * lev.first + k
                p = k if slot == 0 else lev.first + lev.nx + k
                low = pltpu.roll(zq[0, slot], 120 - 8 * x, 1) if x < 15 else zq[0, slot]
                high = pltpu.roll(zq[1, slot], 128 - 8 * x, 1) if x else zq[1, slot]
                e[a, p, :, pl.ds(lev.nz, 128)] = jnp.where(lane < 64, high, low)


def unpack(lev, a_count, a_first, e, zr):
    lane = iota((lev.rows, 128), 1)
    spans = ((0, 0, lev.first), (1, lev.first, lev.nx), (2, lev.first + lev.nx, lev.first))
    for slot, start, count in spans:
        offset = lev.nx - lev.first if slot == 0 else 0
        for k in range(count):
            x = k + offset
            for a in range(a_count):
                low = pltpu.roll(zr[0, slot, a], 120 - 8 * x, 1)
                high = zr[1, slot, a]
                if x:
                    high = pltpu.roll(high, 128 - 8 * x, 1)
                e[a_first + a, start + k, :, pl.ds(lev.nz, 128)] = jnp.where(lane < 64, high, low)


def fine_messages(lev, e, zs, zr, zx, zq):
    first, nx, ny, nz, rows, hy = lev.first, lev.nx, lev.ny, lev.nz, lev.rows, lev.hy
    every, lanes = pl.ds(0, 3), pl.ds(0, nz)

    def planes(dx, skip, w):
        if dx == 0:
            return pl.ds(first, nx), pl.ds(first, nx)
        if dx > 0:
            return pl.ds(first + nx - skip - w, w), pl.ds(first - skip - w, w)
        return pl.ds(first + skip, w), pl.ds(first + nx + skip, w)

    def lines(dy):
        if dy == 0:
            return pl.ds(0, ny), pl.ds(0, ny)
        if dy > 0:
            return pl.ds(ny - hy, hy), pl.ds(rows - hy, hy)
        return pl.ds(0, hy), pl.ds(ny, hy)

    def flat(dx, dy, arrays, skip, w):
        xs, xd = planes(dx, skip, w)
        ys, yd = lines(dy)
        return e.at[arrays, xs, ys, lanes], e.at[arrays, xd, yd, lanes], (dx, dy, 0)

    near, far = [], []
    for dx in (1, -1):
        near.append(flat(dx, 0, pl.ds(0, 1), 0, 3))
        near.append(flat(dx, 0, pl.ds(1, 2), 0, 2))
    for dx in (1, -1):
        for dy in (1, -1):
            near.append(flat(dx, dy, every, 0, 3))
    for dz in (1, -1):
        side = 1 if dz > 0 else 0
        for dx in (1, -1):
            for dy in (0, 1, -1):
                ys, yd = lines(dy)
                xside = 1 if dx > 0 else 0
                near.append((zx.at[side, xside, ys], zq.at[1 - side, 1 - xside, yd], (dx, dy, dz)))
    for dy in (1, -1):
        near.append(flat(0, dy, every, 0, nx))
    for dz in (1, -1):
        side = 1 if dz > 0 else 0
        for dy in (0, 1, -1):
            ys, yd = lines(dy)
            near.append((zs.at[side, :, ys], zr.at[1 - side, :, yd], (0, dy, dz)))
    for dx in (1, -1):
        far.append(flat(dx, 0, pl.ds(0, 1), 3, 2))
        far.append(flat(dx, 0, pl.ds(1, 2), 2, 2))
        for dy in (1, -1):
            far.append(flat(dx, dy, every, 3, 2))
    return near, far


def halo_messages(lev, a_first, a_count, widths, e, zs, zr):
    first, nx, ny, rows, hy = lev.first, lev.nx, lev.ny, lev.rows, lev.hy

    def planes(dx, w):
        if dx == 0:
            return pl.ds(first, nx), pl.ds(first, nx)
        if dx > 0:
            return pl.ds(first + nx - w, w), pl.ds(first - w, w)
        return pl.ds(first, w), pl.ds(first + nx, w)

    def lines(dy):
        if dy == 0:
            return pl.ds(0, ny), pl.ds(0, ny)
        if dy > 0:
            return pl.ds(ny - hy, hy), pl.ds(rows - hy, hy)
        return pl.ds(0, hy), pl.ds(ny, hy)

    found = []
    for dz in (0, -1, 1):
        for dx in (1, -1, 0):
            for dy in (0, 1, -1):
                if dx == dy == dz == 0:
                    continue
                ys, yd = lines(dy)
                if dz == 0:
                    groups = [(a_first, a_count, max(widths))]
                    if dy == 0 and len(widths) > 1:
                        groups = []
                        a = a_first
                        for w, n in ((widths[0], 1), (widths[1], a_count - 1)):
                            groups.append((a, n, w))
                            a += n
                    for a, n, w in groups:
                        xs, xd = planes(dx, w)
                        found.append(
                            (
                                e.at[pl.ds(a, n), xs, ys, pl.ds(0, lev.nz)],
                                e.at[pl.ds(a, n), xd, yd, pl.ds(0, lev.nz)],
                                (dx, dy, dz),
                            )
                        )
                else:
                    side = 1 if dz > 0 else 0
                    slot = 1 - dx
                    found.append(
                        (zs.at[side, :, ys], zr.at[1 - side, slot, :, yd], (dx, dy, dz))
                    )
    return found


GATHER = [
    (dx, 0, dz) for dx in (1, 3, 2, 0) for dz in (0, 1, -1) if (dx, dz) != (0, 0)
]
NEAR = [
    (dx, dy, dz)
    for dx in (-1, 0, 1)
    for dy in (-1, 0, 1)
    for dz in (-1, 0, 1)
    if (dx, dy, dz) != (0, 0, 0)
]
FAR = [(2, 0, 0), (2, 0, 1), (2, 0, -1), (0, 2, 0), (0, -2, 0)]
MESSAGES = 28 + 8 + 26 + 26 + 15 + 15


def kernel(
    sizes, rhs, cond, absb, sol, res,
    e0, fx0, fy0, fz0, inv0, diag0, src0, v0, u0, mask0, miss0, zs0, zr0, zx0, zq0,
    e1, fx1, fy1, fz1, inv1, diag1, src1, v1, u1, mask1, miss1, zs1, zr1, zt1, zu1,
    e2, fx2, fy2, fz2, inv2, diag2, src2, v2, u2, mask2, miss2, own2, gat2,
    e3, fx3, fy3, fz3, inv3, diag3, src3, v3, u3, mask3, miss3,
    p01, p12, p23, s32, s21, s10, tmp, rout, send, recv, local,
):
    gx, gy, gz = (lax.axis_index(axis) for axis in AXES)
    own0 = (pl.ds(L0.first, L0.nx), pl.ds(0, L0.ny), pl.ds(0, L0.nz))
    loads = [
        pltpu.make_async_copy(source, e0.at[(a,) + own0], local.at[a])
        for a, source in enumerate((cond, absb, rhs))
    ]
    for copy in loads:
        copy.start()

    barrier = pltpu.get_barrier_semaphore()
    for offset in NEAR + FAR:
        pl.semaphore_signal(
            barrier, inc=1, device_id=partner(offset, sizes), device_id_type=MESH
        )
    for lev, mask, miss in ((L0, mask0, miss0), (L1, mask1, miss1), (L2, mask2, miss2), (L3, mask3, miss3)):
        make_mask(lev, sizes, mask, miss)
    p01[...] = pool_matrix(L0, L1)[:256, :128]
    p12[...] = pool_matrix(L1, L2)[:128]
    p23[...] = pool_matrix(L2, L3)
    s32[...] = spread_matrix(L3, L2)
    s21[...] = spread_matrix(L2, L1)
    s10[...] = spread_matrix(L1, L0)
    for p in (0, 1, 18, 19):
        for ref in (e2.at[0], v2, u2):
            ref[p] = jnp.zeros((L2.rows, L2.lanes), F32)
    for p in (0, 9):
        for ref in (e3.at[0], v3, u3):
            ref[p] = jnp.zeros((L3.rows, L3.lanes), F32)
    for copy in loads:
        copy.wait()
    pack(L0, 3, 0, e0, zs0)
    pack_edges(L0, zs0, zx0)
    pl.semaphore_wait(barrier, len(NEAR + FAR))

    started = []

    def post(messages):
        copies = []
        for source, target, offset in messages:
            k = len(started)
            copy = pltpu.make_async_remote_copy(
                src_ref=source,
                dst_ref=target,
                send_sem=send.at[k],
                recv_sem=recv.at[k],
                device_id=partner(offset, sizes),
                device_id_type=MESH,
            )
            copy.start()
            started.append(copy)
            copies.append(copy)
        return copies

    def arrive(copies):
        for copy in copies:
            copy.wait_recv()

    def gather_a(a, n):
        x = pl.ds(L2.first + L2.nx * gx, L2.nx)
        return [
            (own2.at[pl.ds(a, n)], gat2.at[1 - offset[2], pl.ds(a, n), x], offset)
            for offset in GATHER
        ]

    def gather_b(a, n):
        x = pl.ds(L2.first, 16)
        mine = e2.at[pl.ds(a, n), x, pl.ds(0, 8)]
        return [
            (mine, e2.at[pl.ds(a, n), x, pl.ds(row, 8)], (0, dy, 0))
            for dy, row in ((1, 40), (-1, 8), (2, 32), (-2, 16))
        ]

    def keep_own(a):
        gat2[1, a, pl.ds(L2.first + L2.nx * gx, L2.nx)] = own2[a]

    def combine(a):
        lane = iota((L2.ny, 128), 1)

        def body(p, carry):
            far = pltpu.roll(jnp.where(lane < 32, gat2[2, a, p], gat2[0, a, p]), 64, 1)
            e2[a, p, pl.ds(0, 8)] = jnp.where(lane < 64, gat2[1, a, p], far)
            return carry

        lax.fori_loop(L2.first, L2.first + 16, body, 0)

    near, far = fine_messages(L0, e0, zs0, zr0, zx0, zq0)
    round_1 = post(near)
    round_f = post(far)

    for a in range(2):

        def stage1(p0, n, a=a):
            for k in range(n):
                q = p0 + k
                p = L0.first + 2 * q
                rows, lanes = pl.ds(0, 32), pl.ds(0, 256)
                stage(tmp, q, e0[a, p, rows, lanes] + e0[a, p + 1, rows, lanes])

        blocks(0, 8, 4, stage1)
        for q, plane in enumerate(pool(tmp, 8, 32, 2, p01)):
            e1[a, L1.first + q, pl.ds(0, 16), pl.ds(0, 128)] = plane
    for a in range(2):
        for q in range(4):
            p = L1.first + 2 * q
            rows, lanes = pl.ds(0, 16), pl.ds(0, 128)
            stage(tmp, 4 * a + q, e1[a, p, rows, lanes] + e1[a, p + 1, rows, lanes])
    for q, plane in enumerate(pool(tmp, 8, 16, 1, p12)):
        own2[q // 4, q % 4] = plane
    keep_own(0)
    keep_own(1)
    round_c2 = post(gather_a(0, 2))
    pack(L1, 2, 0, e1, zs1)
    round_c1 = post(halo_messages(L1, 0, 2, (7,), e1, zs1, zr1))

    base0 = L0.nx * gx - L0.first
    level0 = (fx0, fy0, fz0, inv0)
    arrive(round_1)
    unpack_own(L0, e0, zr0)
    unpack_edges(L0, e0, zq0)

    def build0(lo, hi):
        build(L0, base0, 64, lo, hi, 2, e0, mask0, miss0, *level0, diag0, src0, v0, W[0])

    build0(3, 23)
    arrive(round_c2)
    combine(0)
    combine(1)
    round_d2 = post(gather_b(0, 2))
    sweep(4, 22, 2, src0, *level0, v0, u0, W[1])

    def res0(p):
        return remainder(L0.first + p, src0, fx0, fy0, fz0, diag0, u0)[:32, :256]

    def stage_s1(p0, n):
        for k in range(n):
            q = p0 + k
            stage(tmp, q, res0(2 * q) + res0(2 * q + 1))

    blocks(0, 8, 1, stage_s1)
    for q, plane in enumerate(pool(tmp, 8, 32, 2, p01)):
        e1[2, L1.first + q, pl.ds(0, 16), pl.ds(0, 128)] = plane
    pack(L1, 1, 2, e1, zt1)
    round_2 = post(halo_messages(L1, 2, 1, (6,), e1, zt1, zu1))

    arrive(round_f)
    build0(1, 3)
    build0(23, 25)
    sweep(2, 4, 2, src0, *level0, v0, u0, W[1])
    sweep(22, 24, 2, src0, *level0, v0, u0, W[1])
    base1 = L1.nx * gx - L1.first
    level1 = (fx1, fy1, fz1, inv1)
    arrive(round_c1)
    unpack(L1, 2, 0, e1, zr1)
    build(L1, base1, 32, 1, 21, 4, e1, mask1, miss1, *level1, diag1, src1, v1, None)

    arrive(round_2)
    unpack(L1, 1, 2, e1, zu1)
    first_sweep(L1, base1, 32, 1, 21, 4, e1, mask1, inv1, src1, v1, W[0])
    sweep(2, 20, 3, src1, *level1, v1, u1, W[1])

    def res1(p):
        return remainder(L1.first + p, src1, fx1, fy1, fz1, diag1, u1)[:16, :128]

    for q in range(4):
        stage(tmp, q, res1(2 * q) + res1(2 * q + 1))
    for q, plane in enumerate(pool(tmp, 4, 16, 1, p12)):
        own2[2, q] = plane
    keep_own(2)
    round_3 = post(gather_a(2, 1))

    arrive(round_d2)
    level2 = (fx2, fy2, fz2, inv2)
    level3 = (fx3, fy3, fz3, inv3)
    build(L2, -L2.first, 16, 2, 18, 4, e2, mask2, miss2, *level2, diag2, src2, v2, None)
    for a in range(2):
        for q in range(8):
            stage(tmp, q, e2[a, L2.first + 2 * q] + e2[a, L2.first + 2 * q + 1])
        for q, plane in enumerate(pool(tmp, 8, 48, 1, p23)):
            e3[a, L3.first + q] = plane
    build(L3, -L3.first, 8, 1, 9, 8, e3, mask3, miss3, *level3, diag3, src3, v3, None)

    arrive(round_3)
    combine(2)
    round_4 = post(gather_b(2, 1))
    arrive(round_4)

    first_sweep(L2, -L2.first, 16, 2, 18, 8, e2, mask2, inv2, src2, v2, W[0])
    sweep(2, 18, 4, src2, *level2, v2, u2, W[1])

    def stage_s3(p0, n):
        for k in range(n):
            q = p0 + k
            pair = [remainder(L2.first + 2 * q + j, src2, fx2, fy2, fz2, diag2, u2) for j in (0, 1)]
            stage(tmp, q, pair[0] + pair[1])

    blocks(0, 8, 2, stage_s3)
    for q, plane in enumerate(pool(tmp, 8, 48, 1, p23)):
        e3[2, L3.first + q] = plane
    first_sweep(L3, -L3.first, 8, 1, 9, 8, e3, mask3, inv3, src3, v3, W6[0])
    here, there = v3, u3
    for weight in W6[1:]:
        sweep(1, 9, 8, src3, *level3, here, there, weight)
        here, there = there, here

    spread([here[L3.first + q] for q in range(8)], tmp, s32, 24, 0)
    for q in range(8):
        plane = staged(tmp, q, 48, 1)
        for k in (0, 1):
            u2[L2.first + 2 * q + k] += plane
    sweep(2, 18, 4, src2, *level2, u2, v2, W[0])
    sweep(2, 18, 4, src2, *level2, v2, u2, W[1])

    wide = [u2[L2.nx * gx + q] for q in range(8)]
    wide = [jnp.concatenate([plane[:16], plane[40:]], axis=0) for plane in wide]
    spread(wide, tmp, s21, 16, 4)

    def add1(q0, n):
        for j in range(n):
            plane = staged(tmp, q0 + j, 32, 2)
            for k in (0, 1):
                u1[L1.first - 4 + 2 * (q0 + j) + k] += plane

    blocks(0, 8, 2, add1)
    sweep(4, 18, 7, src1, *level1, u1, v1, W[0])
    sweep(5, 17, 6, src1, *level1, v1, u1, W[1])

    spread([u1[L1.first - 2 + q] for q in range(12)], tmp, s10, 24, 4)

    def add0(q0, n):
        for j in range(n):
            plane = staged(tmp, q0 + j, 48, 3)
            for k in (0, 1):
                u0[L0.first - 4 + 2 * (q0 + j) + k] += plane

    blocks(0, 12, 2, add0)
    sweep(3, 23, 2, src0, *level0, u0, v0, W[0])
    sweep(4, 22, 2, src0, *level0, v0, u0, W[1])
    stores = [pltpu.make_async_copy(u0.at[own0], sol, local.at[3])]
    stores[0].start()

    def last(p0, n):
        for k in range(n):
            rout[p0 + k] = remainder(L0.first + p0 + k, src0, fx0, fy0, fz0, diag0, u0)[:32, :256]

    blocks(0, 16, 2, last)
    stores.append(pltpu.make_async_copy(rout, res, local.at[4]))
    stores[1].start()
    for copy in started:
        copy.wait_send()
    for copy in stores:
        copy.wait()


def solution(mesh):
    sizes = tuple(mesh.shape[axis] for axis in AXES)

    def vmem(*shape):
        return pltpu.VMEM(shape, F32)

    def level(lev):
        return [vmem(3, *lev.shape)] + [vmem(*lev.shape)] * 8 + [vmem(lev.rows, lev.lanes)] * 2

    scratch = [
        *level(L0), vmem(2, 3, 32, 128), vmem(2, 3, 48, 128), vmem(2, 2, 32, 128), vmem(2, 2, 48, 128),
        *level(L1), vmem(2, 2, 16, 128), vmem(2, 3, 2, 32, 128), vmem(2, 1, 16, 128), vmem(2, 3, 1, 32, 128),
        *level(L2), vmem(3, 4, 8, 128), vmem(3, 3, 20, 8, 128),
        *level(L3),
        vmem(256, 128), vmem(128, 128), vmem(128, 128), vmem(128, 128), vmem(128, 256), vmem(256, 384),
        vmem(12, 3, 48, 128), vmem(16, 32, 256),
        pltpu.SemaphoreType.DMA((MESSAGES,)),
        pltpu.SemaphoreType.DMA((MESSAGES,)),
        pltpu.SemaphoreType.DMA((5,)),
    ]

    def cycle(right_side, conductivity, absorption):
        block = jax.ShapeDtypeStruct((16, 32, 256), F32)
        return pl.pallas_call(
            functools.partial(kernel, sizes),
            out_shape=(block, block),
            in_specs=[pl.BlockSpec(memory_space=pl.ANY)] * 3,
            out_specs=(pl.BlockSpec(memory_space=pl.ANY),) * 2,
            scratch_shapes=scratch,
            compiler_params=pltpu.CompilerParams(
                collective_id=0, has_side_effects=True, vmem_limit_bytes=56 * 2**20
            ),
        )(right_side, conductivity, absorption)

    placed = P(*AXES)
    return jax.shard_map(
        cycle, mesh=mesh, in_specs=(placed,) * 3, out_specs=(placed, placed), check_vma=False
    )
```

```python
import functools
import math

import jax
import jax.numpy as jnp
from jax import lax
from jax.experimental import pallas as pl
from jax.experimental.pallas import tpu as pltpu
from jax.sharding import PartitionSpec as P

MESH = pl.DeviceIdType.MESH
AXES = ("gx", "gy", "gz")
EIGEN_LOW = 0.25
EIGEN_HIGH = 2.0
F32 = jnp.float32


def chebyshev_weights(count):
    middle = 0.5 * (EIGEN_HIGH + EIGEN_LOW)
    radius = 0.5 * (EIGEN_HIGH - EIGEN_LOW)
    return [
        1.0 / (middle + radius * math.cos(math.pi * (2 * step + 1) / (2 * count)))
        for step in range(count)
    ]


W = chebyshev_weights(2)
W6 = chebyshev_weights(6)


class Level:
    def __init__(self, scale, own, planes, first, rows, lanes, reach):
        self.scale = scale
        self.nx, self.ny, self.nz = own
        self.planes, self.first = planes, first
        self.rows, self.lanes = rows, lanes
        self.hy, self.hz = reach

    @property
    def shape(self):
        return (self.planes, self.rows, self.lanes)


L0 = Level(1.0, (16, 32, 256), 26, 5, 48, 384, (5, 8))
L1 = Level(0.25, (8, 16, 128), 20, 6, 32, 256, (6, 8))
L2 = Level(0.25**2, (4, 8, 64), 20, 2, 48, 128, (17, 32))
L3 = Level(0.25**3, (2, 4, 32), 10, 1, 24, 128, (8, 16))


def partner(offset, sizes):
    place = []
    for axis, step, size in zip(AXES, offset, sizes):
        index = lax.axis_index(axis)
        place.append(index if step == 0 else lax.rem(index + (step + size), size))
    return tuple(place)


def up(value, axis):
    return pltpu.roll(value, value.shape[axis] - 1, axis)


def down(value, axis):
    return pltpu.roll(value, 1, axis)


def iota(shape, axis):
    return lax.broadcasted_iota(jnp.int32, shape, axis)


def make_mask(lev, sizes, mask_ref, miss_ref):
    shape = (lev.rows, lev.lanes)
    gy, gz = lax.axis_index("gy"), lax.axis_index("gz")
    row, lane = iota(shape, 0), iota(shape, 1)
    y = jnp.where(row < lev.ny + lev.hy, row, row - lev.rows)
    z = jnp.where(lane < lev.nz + lev.hz, lane, lane - lev.lanes)
    yy, zz = y + gy * lev.ny, z + gz * lev.nz
    ymax, zmax = lev.ny * sizes[1], lev.nz * sizes[2]
    good = (y >= -lev.hy) & (z >= -lev.hz) & (yy >= 0) & (yy < ymax) & (zz >= 0) & (zz < zmax)
    mask_ref[...] = jnp.where(good, 1.0, 0.0)
    miss = jnp.where(yy == 0, 1.0, 0.0) + jnp.where(yy == ymax - 1, 1.0, 0.0)
    miss_ref[...] = miss + jnp.where(zz == 0, 1.0, 0.0) + jnp.where(zz == zmax - 1, 1.0, 0.0)


def blocks(lo, hi, step, body):
    full = (hi - lo) // step

    def one(i, carry):
        body(lo + i * step, step)
        return carry

    if full == 1:
        body(lo, step)
    elif full:
        lax.fori_loop(0, full, one, 0)
    if (hi - lo) % step:
        body(lo + full * step, (hi - lo) % step)


def inside(p, base, xmax, mask_ref):
    x = p + base
    return mask_ref[...] > jnp.where((x >= 0) & (x < xmax), 0.5, 2.0)


def build(lev, base, xmax, lo, hi, step, e, mask_ref, miss_ref, fx, fy, fz, inv, diag, src, v, weight):
    scale = lev.scale

    def face(a, b):
        return jnp.where(jnp.minimum(a, b) > 0.0, (0.5 * scale) * (a + b), 0.0)

    def masked(p):
        return jnp.where(inside(p, base, xmax, mask_ref), e[0, p], 0.0)

    fx[lo - 1] = face(masked(lo - 1), masked(lo))

    def body(p0, n):
        cur = masked(p0)
        fxm = fx[p0 - 1]
        for k in range(n):
            p = p0 + k
            x = p + base
            after = masked(p + 1)
            fxp = face(cur, after)
            fx[p] = fxp
            fyp = face(cur, up(cur, 0))
            fy[p] = fyp
            fzp = face(cur, up(cur, 1))
            fz[p] = fzp
            edge = jnp.where(x == 0, 1.0, 0.0) + jnp.where(x == xmax - 1, 1.0, 0.0)
            total = (fxm + fxp) + (fyp + down(fyp, 0)) + (fzp + down(fzp, 1))
            total = total + (scale * cur) * (miss_ref[...] + edge)
            mine = inside(p, base, xmax, mask_ref)
            d = e[1, p] + total
            diag[p] = jnp.where(mine, d, 0.0)
            i = jnp.where(mine, 1.0 / d, 0.0)
            inv[p] = i
            if weight is not None:
                s = jnp.where(mine, e[2, p], 0.0)
                src[p] = s
                v[p] = weight * i * s
            cur, fxm = after, fxp

    blocks(lo, hi, step, body)


def first_sweep(lev, base, xmax, lo, hi, step, e, mask_ref, inv, src, v, weight):
    def body(p0, n):
        for k in range(n):
            p = p0 + k
            s = jnp.where(inside(p, base, xmax, mask_ref), e[2, p], 0.0)
            src[p] = s
            v[p] = weight * inv[p] * s

    blocks(lo, hi, step, body)


def flow(p, v, fx, fy, fz):
    cur = v[p]
    fyp, fzp = fy[p], fz[p]
    total = fx[p] * v[p + 1] + fx[p - 1] * v[p - 1]
    total = total + (fyp * up(cur, 0) + down(fyp * cur, 0))
    return cur, total + (fzp * up(cur, 1) + down(fzp * cur, 1))


def sweep(lo, hi, step, src, fx, fy, fz, inv, v, out, weight):
    def body(p0, n):
        for k in range(n):
            p = p0 + k
            cur, total = flow(p, v, fx, fy, fz)
            out[p] = (1.0 - weight) * cur + (weight * inv[p]) * (src[p] + total)

    blocks(lo, hi, step, body)


def remainder(p, src, fx, fy, fz, diag, v):
    cur, total = flow(p, v, fx, fy, fz)
    return (src[p] - diag[p] * cur) + total


def pool_matrix(fine, coarse):
    shape = (fine.lanes, coarse.lanes)
    f, c = iota(shape, 0), iota(shape, 1)
    zf = jnp.where(f < fine.nz + fine.hz, f, f - fine.lanes)
    zc = jnp.where(c < coarse.nz + coarse.hz, c, c - coarse.lanes)
    hit = (zf >= 2 * zc) & (zf < 2 * zc + 2) & (zc >= -coarse.hz)
    return jnp.where(hit, 0.125, 0.0)


def spread_matrix(coarse, fine):
    shape = (coarse.lanes, fine.lanes)
    c, f = iota(shape, 0), iota(shape, 1)
    zf = jnp.where(f < fine.nz + fine.hz, f, f - fine.lanes)
    zc = jnp.where(c < coarse.nz + coarse.hz, c, c - coarse.lanes)
    hit = (zf >= 2 * zc) & (zf < 2 * zc + 2) & (zf >= -fine.hz)
    return jnp.where(hit, 1.0, 0.0)


def dot(a, b):
    high = a.astype(jnp.bfloat16)
    low = (a - high.astype(F32)).astype(jnp.bfloat16)
    b = b.astype(jnp.bfloat16)
    return jnp.dot(high, b, preferred_element_type=F32) + jnp.dot(low, b, preferred_element_type=F32)


def stage(tmp, q, plane):
    rows, lanes = plane.shape
    for k in range(lanes // 128):
        tmp[q, k, pl.ds(0, rows)] = plane[:, 128 * k : 128 * (k + 1)]


def pool(tmp, count, rows, tiles, matrix):
    parts = []
    for k in range(tiles):
        lines = []
        for q in range(count):
            even = tmp[q, k, pl.ds(0, rows // 2, stride=2)]
            odd = tmp[q, k, pl.ds(1, rows // 2, stride=2)]
            lines.append(even + odd)
        parts.append(jnp.concatenate(lines, axis=0))
    both = parts[0] if tiles == 1 else jnp.concatenate(parts, axis=1)
    done = dot(both, matrix[...])
    return [done[q * (rows // 2) : (q + 1) * (rows // 2)] for q in range(count)]


def spread(planes, tmp, matrix, rows, wrap):
    size = planes[0].shape[0]
    wide = dot(jnp.concatenate(planes, axis=0), matrix[...])
    for q in range(len(planes)):
        for k in range(wide.shape[1] // 128):
            part = wide[q * size : (q + 1) * size, 128 * k : 128 * (k + 1)]
            for odd in (0, 1):
                tmp[q, k, pl.ds(odd, rows - wrap, stride=2)] = part[: rows - wrap]
                if wrap:
                    tmp[q, k, pl.ds(2 * (rows - wrap) + odd, wrap, stride=2)] = part[size - wrap :]


def staged(tmp, q, rows, tiles):
    parts = [tmp[q, k, pl.ds(0, rows)] for k in range(tiles)]
    return parts[0] if tiles == 1 else jnp.concatenate(parts, axis=1)


def pack(lev, a_count, a_first, e, zs):
    shape = (lev.ny, 128)
    group = lax.shift_right_logical(iota(shape, 1), 3)
    for a in range(a_count):
        low = high = jnp.zeros(shape, F32)
        for x in range(lev.nx):
            p = lev.first + x
            lows = e[a_first + a, p, pl.ds(0, lev.ny), pl.ds(0, 128)]
            highs = e[a_first + a, p, pl.ds(0, lev.ny), pl.ds(lev.nz - 128, 128)]
            if x:
                lows = pltpu.roll(lows, 8 * x, 1)
            if x < 15:
                highs = pltpu.roll(highs, 8 * x + 8, 1)
            low = jnp.where(group == x, lows, low)
            high = jnp.where(group == x, highs, high)
        zs[0, a] = low
        zs[1, a] = high


def pack_edges(lev, zs, zx):
    shape = (lev.ny, 128)
    lane = iota(shape, 1)
    width = 8 * lev.first
    for side in (0, 1):
        for xside in (0, 1):
            total = jnp.zeros(shape, F32)
            for a in range(3):
                shift = width * a - (0 if xside == 0 else 128 - width)
                part = zs[side, a]
                if shift % 128:
                    part = pltpu.roll(part, shift % 128, 1)
                total = jnp.where((lane >= width * a) & (lane < width * (a + 1)), part, total)
            zx[side, xside] = total


def unpack_own(lev, e, zr):
    lane = iota((lev.rows, 128), 1)

    def body(x0, n):
        for k in range(n):
            x = x0 + k
            for a in range(3):
                low = pltpu.roll(zr[0, a], 120 - 8 * x, 1)
                high = pltpu.roll(zr[1, a], lax.rem(128 - 8 * x, 128), 1)
                e[a, lev.first + x, :, pl.ds(lev.nz, 128)] = jnp.where(lane < 64, high, low)

    blocks(0, lev.nx, 4, body)


def unpack_edges(lev, e, zq):
    lane = iota((lev.rows, 128), 1)
    for slot in (0, 1):
        for a in range(3):
            for k in range(lev.first):
                x = a * lev.first + k
                p = k if slot == 0 else lev.first + lev.nx + k
                low = pltpu.roll(zq[0, slot], 120 - 8 * x, 1) if x < 15 else zq[0, slot]
                high = pltpu.roll(zq[1, slot], 128 - 8 * x, 1) if x else zq[1, slot]
                e[a, p, :, pl.ds(lev.nz, 128)] = jnp.where(lane < 64, high, low)


def unpack(lev, a_count, a_first, e, zr):
    lane = iota((lev.rows, 128), 1)
    spans = ((0, 0, lev.first), (1, lev.first, lev.nx), (2, lev.first + lev.nx, lev.first))
    for slot, start, count in spans:
        offset = lev.nx - lev.first if slot == 0 else 0
        for k in range(count):
            x = k + offset
            for a in range(a_count):
                low = pltpu.roll(zr[0, slot, a], 120 - 8 * x, 1)
                high = zr[1, slot, a]
                if x:
                    high = pltpu.roll(high, 128 - 8 * x, 1)
                e[a_first + a, start + k, :, pl.ds(lev.nz, 128)] = jnp.where(lane < 64, high, low)


def fine_messages(lev, e, zs, zr, zx, zq, edges):
    first, nx, ny, nz, rows, hy = lev.first, lev.nx, lev.ny, lev.nz, lev.rows, lev.hy
    every, lanes = pl.ds(0, 3), pl.ds(0, nz)

    def planes(dx, skip, w):
        if dx == 0:
            return pl.ds(first, nx), pl.ds(first, nx)
        if dx > 0:
            return pl.ds(first + nx - skip - w, w), pl.ds(first - skip - w, w)
        return pl.ds(first + skip, w), pl.ds(first + nx + skip, w)

    def lines(dy, skip=0, w=hy):
        if dy == 0:
            return pl.ds(0, ny), pl.ds(0, ny)
        if dy > 0:
            return pl.ds(ny - skip - w, w), pl.ds(rows - skip - w, w)
        return pl.ds(skip, w), pl.ds(ny + skip, w)

    def flat(dx, dy, arrays, x_part, y_part=(0, hy)):
        xs, xd = planes(dx, *x_part)
        ys, yd = lines(dy, *y_part)
        return e.at[arrays, xs, ys, lanes], e.at[arrays, xd, yd, lanes], (dx, dy, 0)

    near_x, near_yz, far = [], [], []
    for dx in (1, -1):
        near_x.append(flat(dx, 0, pl.ds(0, 1), (0, 3)))
        near_x.append(flat(dx, 0, pl.ds(1, 2), (0, 2)))
    for dx in (1, -1):
        for dy in (1, -1):
            near_x.append(flat(dx, dy, every, (0, 2), (0, 2)))
    for dz in (1, -1):
        side = 1 if dz > 0 else 0
        for dx in (1, -1):
            for dy in (0, 1, -1):
                ys, yd = lines(dy)
                xside = 1 if dx > 0 else 0
                near_x.append((zx.at[side, xside, ys], zq.at[1 - side, 1 - xside, yd], (dx, dy, dz)))
    for dy in (1, -1):
        near_yz.append(flat(0, dy, every, (0, nx)))
    for dz in (1, -1):
        side = 1 if dz > 0 else 0
        for dy in (0, 1, -1):
            ys, yd = lines(dy)
            near_yz.append((zs.at[side, :, ys], zr.at[1 - side, :, yd], (0, dy, dz)))
    for dx in (1, -1):
        far.append(flat(dx, 0, pl.ds(0, 1), (3, 2)))
        far.append(flat(dx, 0, pl.ds(1, 2), (2, 2)))
        for dy in (1, -1):
            xs, ys = planes(dx, 0, 5)[0], lines(dy)[0]
            low = 1 if dy > 0 else 0
            place = (2 if dx < 0 else 0) + low
            far.append((e.at[every, xs, ys, lanes], edges.at[place, :, :, pl.ds(3 * low, hy)], (dx, dy, 0)))
    return near_x, near_yz, far


def halo_messages(lev, a_first, a_count, widths, e, zs, zr):
    first, nx, ny, rows, hy = lev.first, lev.nx, lev.ny, lev.rows, lev.hy

    def planes(dx, w):
        if dx == 0:
            return pl.ds(first, nx), pl.ds(first, nx)
        if dx > 0:
            return pl.ds(first + nx - w, w), pl.ds(first - w, w)
        return pl.ds(first, w), pl.ds(first + nx, w)

    def lines(dy):
        if dy == 0:
            return pl.ds(0, ny), pl.ds(0, ny)
        if dy > 0:
            return pl.ds(ny - hy, hy), pl.ds(rows - hy, hy)
        return pl.ds(0, hy), pl.ds(ny, hy)

    found = []
    for dz in (0, -1, 1):
        for dx in (1, -1, 0):
            for dy in (0, 1, -1):
                if dx == dy == dz == 0:
                    continue
                ys, yd = lines(dy)
                if dz == 0:
                    groups = [(a_first, a_count, max(widths))]
                    if dy == 0 and len(widths) > 1:
                        groups = []
                        a = a_first
                        for w, n in ((widths[0], 1), (widths[1], a_count - 1)):
                            groups.append((a, n, w))
                            a += n
                    for a, n, w in groups:
                        xs, xd = planes(dx, w)
                        found.append(
                            (
                                e.at[pl.ds(a, n), xs, ys, pl.ds(0, lev.nz)],
                                e.at[pl.ds(a, n), xd, yd, pl.ds(0, lev.nz)],
                                (dx, dy, dz),
                            )
                        )
                else:
                    side = 1 if dz > 0 else 0
                    slot = 1 - dx
                    found.append(
                        (zs.at[side, :, ys], zr.at[1 - side, slot, :, yd], (dx, dy, dz))
                    )
    return found


GATHER = [
    (dx, 0, dz) for dx in (1, 3, 2, 0) for dz in (0, 1, -1) if (dx, dz) != (0, 0)
]
NEAR = [
    (dx, dy, dz)
    for dx in (-1, 0, 1)
    for dy in (-1, 0, 1)
    for dz in (-1, 0, 1)
    if (dx, dy, dz) != (0, 0, 0)
]
FAR = [(2, 0, 0), (2, 0, 1), (2, 0, -1), (0, 2, 0), (0, -2, 0), (0, 3, 0), (0, -3, 0)]
MESSAGES = 28 + 8 + 26 + 26 + 11 + 6 + 11 + 4


def kernel(
    sizes, rhs, cond, absb, sol, res,
    e0, fx0, fy0, fz0, inv0, diag0, src0, v0, u0, mask0, miss0, zs0, zr0, zx0, zq0, edges0,
    e1, fx1, fy1, fz1, inv1, diag1, src1, v1, u1, mask1, miss1, zs1, zr1, zt1, zu1,
    e2, fx2, fy2, fz2, inv2, diag2, src2, v2, u2, mask2, miss2, own2, cut2, gatc, gats, gatz,
    e3, fx3, fy3, fz3, inv3, diag3, src3, v3, u3, mask3, miss3,
    p01, p12, p23, s32, s21, s10, tmp, rout, send, recv, local,
):
    gx, gy, gz = (lax.axis_index(axis) for axis in AXES)
    own0 = (pl.ds(L0.first, L0.nx), pl.ds(0, L0.ny), pl.ds(0, L0.nz))
    loads = [
        pltpu.make_async_copy(source, e0.at[(a,) + own0], local.at[a])
        for a, source in enumerate((cond, absb, rhs))
    ]
    for copy in loads:
        copy.start()

    barrier = pltpu.get_barrier_semaphore()
    for offset in NEAR + FAR:
        pl.semaphore_signal(
            barrier, inc=1, device_id=partner(offset, sizes), device_id_type=MESH
        )
    for copy in loads:
        copy.wait()
    pack(L0, 3, 0, e0, zs0)
    pack_edges(L0, zs0, zx0)
    pl.semaphore_wait(barrier, len(NEAR + FAR))

    started = []

    def post(messages):
        copies = []
        for source, target, offset in messages:
            k = len(started)
            copy = pltpu.make_async_remote_copy(
                src_ref=source,
                dst_ref=target,
                send_sem=send.at[k],
                recv_sem=recv.at[k],
                device_id=partner(offset, sizes),
                device_id_type=MESH,
            )
            copy.start()
            started.append(copy)
            copies.append(copy)
        return copies

    def arrive(copies):
        for copy in copies:
            copy.wait_recv()

    def gather_a(arrays, gat):
        lane = iota((L2.ny, 128), 1)
        group = lax.shift_right_logical(lane, 5)
        for a in arrays:
            low = high = jnp.zeros((L2.ny, 128), F32)
            for q in range(4):
                plane = own2[a, q]
                low = jnp.where(group == q, pltpu.roll(plane, 32 * q, 1) if q else plane, low)
                high = jnp.where(group == q, pltpu.roll(plane, 32 * q - 32, 1) if q > 1 else (plane if q else pltpu.roll(plane, 96, 1)), high)
            cut2[0, a] = low
            cut2[1, a] = high
        if len(arrays) == 2:
            for q in range(4):
                own2[3, q] = jnp.where(lane < 64, own2[0, q], pltpu.roll(own2[1, q], 64, 1))
        whole = 3 if len(arrays) == 2 else arrays[0]
        first = pl.ds(arrays[0], len(arrays))
        mine = pl.ds(L2.nx * gx, L2.nx)
        gat[mine] = own2[whole]
        messages = []
        for dx, dy, dz in GATHER:
            if dz == 0:
                messages.append((own2.at[whole], gat.at[mine], (dx, dy, dz)))
            else:
                side = 1 if dz > 0 else 0
                messages.append((cut2.at[side, first], gatz.at[side, gx, first], (dx, dy, dz)))
        return messages

    def combine(a, gat):
        lane = iota((L2.ny, 128), 1)
        for p in range(16):
            q = p % 4
            far = pltpu.roll(gatz[0, p // 4, a], (64 - 32 * q) % 128, 1) if q != 2 else gatz[0, p // 4, a]
            low = pltpu.roll(gatz[1, p // 4, a], (96 - 32 * q) % 128, 1) if q != 3 else gatz[1, p // 4, a]
            mine = pltpu.roll(gat[p], 64, 1) if a == 1 else gat[p]
            e2[a, L2.first + p, pl.ds(0, 8)] = jnp.where(lane < 64, mine, jnp.where(lane < 96, far, low))

    def gather_b(a, n):
        x = pl.ds(L2.first, 16)
        mine = e2.at[pl.ds(a, n), x, pl.ds(0, 8)]
        messages = [
            (mine, e2.at[pl.ds(a, n), x, pl.ds(row, 8)], (0, dy, 0))
            for dy, row in ((1, 40), (-1, 8), (2, 32), (-2, 16))
        ]
        if a == 0:
            for dy, row, to in ((3, 7, 31), (-3, 0, 24)):
                messages.append(
                    (e2.at[pl.ds(0, 1), x, pl.ds(row, 1)], e2.at[pl.ds(0, 1), x, pl.ds(to, 1)], (0, dy, 0))
                )
        return messages

    near_x, near_yz, far = fine_messages(L0, e0, zs0, zr0, zx0, zq0, edges0)
    round_1x = post(near_x)
    round_1 = post(near_yz)
    for lev, mask, miss in ((L0, mask0, miss0), (L1, mask1, miss1), (L2, mask2, miss2), (L3, mask3, miss3)):
        make_mask(lev, sizes, mask, miss)
    p01[...] = pool_matrix(L0, L1)[:256, :128]
    p12[...] = pool_matrix(L1, L2)[:128]
    p23[...] = pool_matrix(L2, L3)
    s32[...] = spread_matrix(L3, L2)
    s21[...] = spread_matrix(L2, L1)
    s10[...] = spread_matrix(L1, L0)
    for p in (0, 1, 18, 19):
        for ref in (e2.at[0], v2, u2):
            ref[p] = jnp.zeros((L2.rows, L2.lanes), F32)
    e2[1, pl.ds(2, 16), pl.ds(24, 8)] = jnp.ones((16, 8, 128), F32)
    e2[2, pl.ds(2, 16), pl.ds(24, 8)] = jnp.zeros((16, 8, 128), F32)
    for p in (0, 9):
        for ref in (e3.at[0], v3, u3):
            ref[p] = jnp.zeros((L3.rows, L3.lanes), F32)

    for a in range(2):

        def stage1(p0, n, a=a):
            for k in range(n):
                q = p0 + k
                p = L0.first + 2 * q
                rows, lanes = pl.ds(0, 32), pl.ds(0, 256)
                stage(tmp, q, e0[a, p, rows, lanes] + e0[a, p + 1, rows, lanes])

        blocks(0, 8, 4, stage1)
        for q, plane in enumerate(pool(tmp, 8, 32, 2, p01)):
            e1[a, L1.first + q, pl.ds(0, 16), pl.ds(0, 128)] = plane
    for a in range(2):
        for q in range(4):
            p = L1.first + 2 * q
            rows, lanes = pl.ds(0, 16), pl.ds(0, 128)
            stage(tmp, 4 * a + q, e1[a, p, rows, lanes] + e1[a, p + 1, rows, lanes])
    for q, plane in enumerate(pool(tmp, 8, 16, 1, p12)):
        own2[q // 4, q % 4] = plane
    round_c2 = post(gather_a((0, 1), gatc))
    pack(L1, 2, 0, e1, zs1)
    round_c1 = post(halo_messages(L1, 0, 2, (6,), e1, zs1, zr1))

    base0 = L0.nx * gx - L0.first
    level0 = (fx0, fy0, fz0, inv0)
    arrive(round_1)
    unpack_own(L0, e0, zr0)

    def build0(lo, hi, step=2):
        build(L0, base0, 64, lo, hi, step, e0, mask0, miss0, *level0, diag0, src0, v0, W[0])

    build0(6, 20)
    sweep(7, 19, 2, src0, *level0, v0, u0, W[1])
    arrive(round_1x)
    unpack_edges(L0, e0, zq0)
    build0(3, 6, 3)
    build0(20, 23, 3)
    sweep(4, 7, 3, src0, *level0, v0, u0, W[1])
    sweep(19, 22, 3, src0, *level0, v0, u0, W[1])

    def res0(p):
        return remainder(L0.first + p, src0, fx0, fy0, fz0, diag0, u0)[:32, :256]

    def stage_s1(p0, n):
        for k in range(n):
            q = p0 + k
            stage(tmp, q, res0(2 * q) + res0(2 * q + 1))

    blocks(0, 8, 1, stage_s1)
    for q, plane in enumerate(pool(tmp, 8, 32, 2, p01)):
        e1[2, L1.first + q, pl.ds(0, 16), pl.ds(0, 128)] = plane
    pack(L1, 1, 2, e1, zt1)
    round_2 = post(halo_messages(L1, 2, 1, (5,), e1, zt1, zu1))
    round_f = post(far)

    arrive(round_c2)
    combine(0, gatc)
    combine(1, gatc)
    round_d2 = post(gather_b(0, 2))
    base1 = L1.nx * gx - L1.first
    level1 = (fx1, fy1, fz1, inv1)
    arrive(round_c1)
    unpack(L1, 2, 0, e1, zr1)
    build(L1, base1, 32, 1, 19, 3, e1, mask1, miss1, *level1, diag1, src1, v1, None)

    arrive(round_2)
    unpack(L1, 1, 2, e1, zu1)
    first_sweep(L1, base1, 32, 1, 19, 6, e1, mask1, inv1, src1, v1, W[0])
    sweep(2, 18, 4, src1, *level1, v1, u1, W[1])

    def res1(p):
        return remainder(L1.first + p, src1, fx1, fy1, fz1, diag1, u1)[:16, :128]

    for q in range(4):
        stage(tmp, q, res1(2 * q) + res1(2 * q + 1))
    for q, plane in enumerate(pool(tmp, 4, 16, 1, p12)):
        own2[2, q] = plane
    round_3 = post(gather_a((2,), gats))

    arrive(round_d2)
    level2 = (fx2, fy2, fz2, inv2)
    level3 = (fx3, fy3, fz3, inv3)
    build(L2, -L2.first, 16, 2, 18, 4, e2, mask2, miss2, *level2, diag2, src2, v2, None)
    for a in range(2):
        for q in range(8):
            stage(tmp, q, e2[a, L2.first + 2 * q] + e2[a, L2.first + 2 * q + 1])
        for q, plane in enumerate(pool(tmp, 8, 48, 1, p23)):
            e3[a, L3.first + q] = plane
    build(L3, -L3.first, 8, 1, 9, 8, e3, mask3, miss3, *level3, diag3, src3, v3, None)

    arrive(round_3)
    combine(2, gats)
    round_4 = post(gather_b(2, 1))

    arrive(round_f)
    for place in range(4):
        for k in range(5):
            p = k if place < 2 else 21 + k
            for a in range(3):
                e0[a, p, pl.ds(40 if place % 2 else 32, 8), pl.ds(0, 256)] = edges0[place, a, k]
    build0(1, 6, 5)
    build0(20, 25, 5)
    sweep(2, 7, 5, src0, *level0, v0, u0, W[1])
    sweep(19, 24, 5, src0, *level0, v0, u0, W[1])
    arrive(round_4)

    first_sweep(L2, -L2.first, 16, 2, 18, 8, e2, mask2, inv2, src2, v2, W[0])
    sweep(2, 18, 4, src2, *level2, v2, u2, W[1])

    def stage_s3(p0, n):
        for k in range(n):
            q = p0 + k
            pair = [remainder(L2.first + 2 * q + j, src2, fx2, fy2, fz2, diag2, u2) for j in (0, 1)]
            stage(tmp, q, pair[0] + pair[1])

    blocks(0, 8, 2, stage_s3)
    for q, plane in enumerate(pool(tmp, 8, 48, 1, p23)):
        e3[2, L3.first + q] = plane
    first_sweep(L3, -L3.first, 8, 1, 9, 8, e3, mask3, inv3, src3, v3, W6[0])
    here, there = v3, u3
    for weight in W6[1:]:
        sweep(1, 9, 8, src3, *level3, here, there, weight)
        here, there = there, here

    spread([here[L3.first + q] for q in range(8)], tmp, s32, 24, 0)
    for q in range(8):
        plane = staged(tmp, q, 48, 1)
        for k in (0, 1):
            u2[L2.first + 2 * q + k] += plane
    sweep(2, 18, 4, src2, *level2, u2, v2, W[0])
    sweep(2, 18, 4, src2, *level2, v2, u2, W[1])

    wide = [u2[L2.nx * gx + q] for q in range(8)]
    wide = [jnp.concatenate([plane[:16], plane[40:]], axis=0) for plane in wide]
    spread(wide, tmp, s21, 16, 4)

    def add1(q0, n):
        for j in range(n):
            plane = staged(tmp, q0 + j, 32, 2)
            for k in (0, 1):
                u1[L1.first - 4 + 2 * (q0 + j) + k] += plane

    blocks(0, 8, 2, add1)
    sweep(3, 17, 7, src1, *level1, u1, v1, W[0])
    sweep(4, 16, 6, src1, *level1, v1, u1, W[1])

    spread([u1[L1.first - 2 + q] for q in range(12)], tmp, s10, 24, 4)

    def add0(q0, n):
        for j in range(n):
            plane = staged(tmp, q0 + j, 48, 3)
            for k in (0, 1):
                u0[L0.first - 4 + 2 * (q0 + j) + k] += plane

    blocks(0, 12, 2, add0)
    sweep(3, 23, 2, src0, *level0, u0, v0, W[0])
    sweep(4, 22, 2, src0, *level0, v0, u0, W[1])
    stores = [pltpu.make_async_copy(u0.at[own0], sol, local.at[3])]
    stores[0].start()

    def last(p0, n):
        for k in range(n):
            rout[p0 + k] = remainder(L0.first + p0 + k, src0, fx0, fy0, fz0, diag0, u0)[:32, :256]

    blocks(0, 16, 2, last)
    stores.append(pltpu.make_async_copy(rout, res, local.at[4]))
    stores[1].start()
    for copy in started:
        copy.wait_send()
    for copy in stores:
        copy.wait()


def solution(mesh):
    sizes = tuple(mesh.shape[axis] for axis in AXES)

    def vmem(*shape):
        return pltpu.VMEM(shape, F32)

    def level(lev):
        return [vmem(3, *lev.shape)] + [vmem(*lev.shape)] * 8 + [vmem(lev.rows, lev.lanes)] * 2

    scratch = [
        *level(L0), vmem(2, 3, 32, 128), vmem(2, 3, 48, 128), vmem(2, 2, 32, 128), vmem(2, 2, 48, 128), vmem(4, 3, 5, 8, 256),
        *level(L1), vmem(2, 2, 16, 128), vmem(2, 3, 2, 32, 128), vmem(2, 1, 16, 128), vmem(2, 3, 1, 32, 128),
        *level(L2), vmem(4, 4, 8, 128), vmem(2, 3, 8, 128), vmem(16, 8, 128), vmem(16, 8, 128), vmem(2, 4, 3, 8, 128),
        *level(L3),
        vmem(256, 128), vmem(128, 128), vmem(128, 128), vmem(128, 128), vmem(128, 256), vmem(256, 384),
        vmem(12, 3, 48, 128), vmem(16, 32, 256),
        pltpu.SemaphoreType.DMA((MESSAGES,)),
        pltpu.SemaphoreType.DMA((MESSAGES,)),
        pltpu.SemaphoreType.DMA((5,)),
    ]

    def cycle(right_side, conductivity, absorption):
        block = jax.ShapeDtypeStruct((16, 32, 256), F32)
        return pl.pallas_call(
            functools.partial(kernel, sizes),
            out_shape=(block, block),
            in_specs=[pl.BlockSpec(memory_space=pl.ANY)] * 3,
            out_specs=(pl.BlockSpec(memory_space=pl.ANY),) * 2,
            scratch_shapes=scratch,
            compiler_params=pltpu.CompilerParams(
                collective_id=0, has_side_effects=True, vmem_limit_bytes=56 * 2**20
            ),
        )(right_side, conductivity, absorption)

    placed = P(*AXES)
    return jax.shard_map(
        cycle, mesh=mesh, in_specs=(placed,) * 3, out_specs=(placed, placed), check_vma=False
    )
```

```python
import functools
import math

import jax
import jax.numpy as jnp
from jax import lax
from jax.experimental import pallas as pl
from jax.experimental.pallas import tpu as pltpu
from jax.sharding import PartitionSpec as P

MESH = pl.DeviceIdType.MESH
AXES = ("gx", "gy", "gz")
EIGEN_LOW = 0.25
EIGEN_HIGH = 2.0
F32 = jnp.float32


def chebyshev_weights(count):
    middle = 0.5 * (EIGEN_HIGH + EIGEN_LOW)
    radius = 0.5 * (EIGEN_HIGH - EIGEN_LOW)
    return [
        1.0 / (middle + radius * math.cos(math.pi * (2 * step + 1) / (2 * count)))
        for step in range(count)
    ]


W = chebyshev_weights(2)
W6 = chebyshev_weights(6)


class Level:
    def __init__(self, scale, own, planes, first, rows, lanes, reach):
        self.scale = scale
        self.nx, self.ny, self.nz = own
        self.planes, self.first = planes, first
        self.rows, self.lanes = rows, lanes
        self.hy, self.hz = reach

    @property
    def shape(self):
        return (self.planes, self.rows, self.lanes)


L0 = Level(1.0, (16, 32, 256), 26, 5, 48, 384, (5, 8))
L1 = Level(0.25, (8, 16, 128), 20, 6, 32, 256, (6, 8))
L2 = Level(0.25**2, (4, 8, 64), 20, 2, 48, 128, (17, 32))
L3 = Level(0.25**3, (2, 4, 32), 10, 1, 24, 128, (8, 16))


def partner(offset, sizes):
    place = []
    for axis, step, size in zip(AXES, offset, sizes):
        index = lax.axis_index(axis)
        place.append(index if step == 0 else lax.rem(index + (step + size), size))
    return tuple(place)


def up(value, axis):
    return pltpu.roll(value, value.shape[axis] - 1, axis)


def down(value, axis):
    return pltpu.roll(value, 1, axis)


def iota(shape, axis):
    return lax.broadcasted_iota(jnp.int32, shape, axis)


def make_mask(lev, sizes, mask_ref, miss_ref):
    shape = (lev.rows, lev.lanes)
    gy, gz = lax.axis_index("gy"), lax.axis_index("gz")
    row, lane = iota(shape, 0), iota(shape, 1)
    y = jnp.where(row < lev.ny + lev.hy, row, row - lev.rows)
    z = jnp.where(lane < lev.nz + lev.hz, lane, lane - lev.lanes)
    yy, zz = y + gy * lev.ny, z + gz * lev.nz
    ymax, zmax = lev.ny * sizes[1], lev.nz * sizes[2]
    good = (y >= -lev.hy) & (z >= -lev.hz) & (yy >= 0) & (yy < ymax) & (zz >= 0) & (zz < zmax)
    mask_ref[...] = jnp.where(good, 1.0, 0.0)
    miss = jnp.where(yy == 0, 1.0, 0.0) + jnp.where(yy == ymax - 1, 1.0, 0.0)
    miss_ref[...] = miss + jnp.where(zz == 0, 1.0, 0.0) + jnp.where(zz == zmax - 1, 1.0, 0.0)


def blocks(lo, hi, step, body):
    full = (hi - lo) // step

    def one(i, carry):
        body(lo + i * step, step)
        return carry

    if full == 1:
        body(lo, step)
    elif full:
        lax.fori_loop(0, full, one, 0)
    if (hi - lo) % step:
        body(lo + full * step, (hi - lo) % step)


def inside(p, base, xmax, mask_ref):
    x = p + base
    return mask_ref[...] > jnp.where((x >= 0) & (x < xmax), 0.5, 2.0)


def build(lev, base, xmax, lo, hi, step, e, mask_ref, miss_ref, fx, fy, fz, inv, diag, src, v, weight):
    scale = lev.scale

    def face(a, b):
        return jnp.where(jnp.minimum(a, b) > 0.0, (0.5 * scale) * (a + b), 0.0)

    def masked(p):
        return jnp.where(inside(p, base, xmax, mask_ref), e[0, p], 0.0)

    fx[lo - 1] = face(masked(lo - 1), masked(lo))

    def body(p0, n):
        cur = masked(p0)
        fxm = fx[p0 - 1]
        for k in range(n):
            p = p0 + k
            x = p + base
            after = masked(p + 1)
            fxp = face(cur, after)
            fx[p] = fxp
            fyp = face(cur, up(cur, 0))
            fy[p] = fyp
            fzp = face(cur, up(cur, 1))
            fz[p] = fzp
            edge = jnp.where(x == 0, 1.0, 0.0) + jnp.where(x == xmax - 1, 1.0, 0.0)
            total = (fxm + fxp) + (fyp + down(fyp, 0)) + (fzp + down(fzp, 1))
            total = total + (scale * cur) * (miss_ref[...] + edge)
            mine = inside(p, base, xmax, mask_ref)
            d = e[1, p] + total
            diag[p] = jnp.where(mine, d, 0.0)
            i = jnp.where(mine, 1.0 / d, 0.0)
            inv[p] = i
            if weight is not None:
                s = jnp.where(mine, e[2, p], 0.0)
                src[p] = s
                v[p] = weight * i * s
            cur, fxm = after, fxp

    blocks(lo, hi, step, body)


def first_sweep(lev, base, xmax, lo, hi, step, e, mask_ref, inv, src, v, weight):
    def body(p0, n):
        for k in range(n):
            p = p0 + k
            s = jnp.where(inside(p, base, xmax, mask_ref), e[2, p], 0.0)
            src[p] = s
            v[p] = weight * inv[p] * s

    blocks(lo, hi, step, body)


def flow(p, v, fx, fy, fz):
    cur = v[p]
    fyp, fzp = fy[p], fz[p]
    total = fx[p] * v[p + 1] + fx[p - 1] * v[p - 1]
    total = total + (fyp * up(cur, 0) + down(fyp * cur, 0))
    return cur, total + (fzp * up(cur, 1) + down(fzp * cur, 1))


def sweep(lo, hi, step, src, fx, fy, fz, inv, v, out, weight):
    def body(p0, n):
        for k in range(n):
            p = p0 + k
            cur, total = flow(p, v, fx, fy, fz)
            out[p] = (1.0 - weight) * cur + (weight * inv[p]) * (src[p] + total)

    blocks(lo, hi, step, body)


def remainder(p, src, fx, fy, fz, diag, v):
    cur, total = flow(p, v, fx, fy, fz)
    return (src[p] - diag[p] * cur) + total


def pool_matrix(fine, coarse):
    shape = (fine.lanes, coarse.lanes)
    f, c = iota(shape, 0), iota(shape, 1)
    zf = jnp.where(f < fine.nz + fine.hz, f, f - fine.lanes)
    zc = jnp.where(c < coarse.nz + coarse.hz, c, c - coarse.lanes)
    hit = (zf >= 2 * zc) & (zf < 2 * zc + 2) & (zc >= -coarse.hz)
    return jnp.where(hit, 0.125, 0.0)


def spread_matrix(coarse, fine):
    shape = (coarse.lanes, fine.lanes)
    c, f = iota(shape, 0), iota(shape, 1)
    zf = jnp.where(f < fine.nz + fine.hz, f, f - fine.lanes)
    zc = jnp.where(c < coarse.nz + coarse.hz, c, c - coarse.lanes)
    hit = (zf >= 2 * zc) & (zf < 2 * zc + 2) & (zf >= -fine.hz)
    return jnp.where(hit, 1.0, 0.0)


def dot(a, b):
    high = a.astype(jnp.bfloat16)
    low = (a - high.astype(F32)).astype(jnp.bfloat16)
    b = b.astype(jnp.bfloat16)
    return jnp.dot(high, b, preferred_element_type=F32) + jnp.dot(low, b, preferred_element_type=F32)


def stage(tmp, q, plane):
    rows, lanes = plane.shape
    for k in range(lanes // 128):
        tmp[q, k, pl.ds(0, rows)] = plane[:, 128 * k : 128 * (k + 1)]


def pool(tmp, count, rows, tiles, matrix):
    parts = []
    for k in range(tiles):
        lines = []
        for q in range(count):
            even = tmp[q, k, pl.ds(0, rows // 2, stride=2)]
            odd = tmp[q, k, pl.ds(1, rows // 2, stride=2)]
            lines.append(even + odd)
        parts.append(jnp.concatenate(lines, axis=0))
    both = parts[0] if tiles == 1 else jnp.concatenate(parts, axis=1)
    done = dot(both, matrix[...])
    return [done[q * (rows // 2) : (q + 1) * (rows // 2)] for q in range(count)]


def spread(planes, tmp, matrix, rows, wrap):
    size = planes[0].shape[0]
    wide = dot(jnp.concatenate(planes, axis=0), matrix[...])
    for q in range(len(planes)):
        for k in range(wide.shape[1] // 128):
            part = wide[q * size : (q + 1) * size, 128 * k : 128 * (k + 1)]
            for odd in (0, 1):
                tmp[q, k, pl.ds(odd, rows - wrap, stride=2)] = part[: rows - wrap]
                if wrap:
                    tmp[q, k, pl.ds(2 * (rows - wrap) + odd, wrap, stride=2)] = part[size - wrap :]


def staged(tmp, q, rows, tiles):
    parts = [tmp[q, k, pl.ds(0, rows)] for k in range(tiles)]
    return parts[0] if tiles == 1 else jnp.concatenate(parts, axis=1)


def pack(lev, a_count, a_first, e, zs):
    shape = (lev.ny, 128)
    group = lax.shift_right_logical(iota(shape, 1), 3)
    for a in range(a_count):
        low = high = jnp.zeros(shape, F32)
        for x in range(lev.nx):
            p = lev.first + x
            lows = e[a_first + a, p, pl.ds(0, lev.ny), pl.ds(0, 128)]
            highs = e[a_first + a, p, pl.ds(0, lev.ny), pl.ds(lev.nz - 128, 128)]
            if x:
                lows = pltpu.roll(lows, 8 * x, 1)
            if x < 15:
                highs = pltpu.roll(highs, 8 * x + 8, 1)
            low = jnp.where(group == x, lows, low)
            high = jnp.where(group == x, highs, high)
        zs[0, a] = low
        zs[1, a] = high


def pack_edges(lev, zs, zx):
    shape = (lev.ny, 128)
    lane = iota(shape, 1)
    width = 8 * lev.first
    for side in (0, 1):
        for xside in (0, 1):
            total = jnp.zeros(shape, F32)
            for a in range(3):
                shift = width * a - (0 if xside == 0 else 128 - width)
                part = zs[side, a]
                if shift % 128:
                    part = pltpu.roll(part, shift % 128, 1)
                total = jnp.where((lane >= width * a) & (lane < width * (a + 1)), part, total)
            zx[side, xside] = total


def unpack_own(lev, e, zr):
    lane = iota((lev.rows, 128), 1)

    def body(x0, n):
        for k in range(n):
            x = x0 + k
            for a in range(3):
                low = pltpu.roll(zr[0, a], 120 - 8 * x, 1)
                high = pltpu.roll(zr[1, a], lax.rem(128 - 8 * x, 128), 1)
                e[a, lev.first + x, :, pl.ds(lev.nz, 128)] = jnp.where(lane < 64, high, low)

    blocks(0, lev.nx, 4, body)


def unpack_edges(lev, e, zq):
    lane = iota((lev.rows, 128), 1)
    for slot in (0, 1):
        for a in range(3):
            for k in range(lev.first):
                x = a * lev.first + k
                p = k if slot == 0 else lev.first + lev.nx + k
                low = pltpu.roll(zq[0, slot], 120 - 8 * x, 1) if x < 15 else zq[0, slot]
                high = pltpu.roll(zq[1, slot], 128 - 8 * x, 1) if x else zq[1, slot]
                e[a, p, :, pl.ds(lev.nz, 128)] = jnp.where(lane < 64, high, low)


def unpack(lev, a_count, a_first, e, zr):
    lane = iota((lev.rows, 128), 1)
    spans = ((0, 0, lev.first), (1, lev.first, lev.nx), (2, lev.first + lev.nx, lev.first))
    for slot, start, count in spans:
        offset = lev.nx - lev.first if slot == 0 else 0
        for k in range(count):
            x = k + offset
            for a in range(a_count):
                low = pltpu.roll(zr[0, slot, a], 120 - 8 * x, 1)
                high = zr[1, slot, a]
                if x:
                    high = pltpu.roll(high, 128 - 8 * x, 1)
                e[a_first + a, start + k, :, pl.ds(lev.nz, 128)] = jnp.where(lane < 64, high, low)


def fine_messages(lev, inputs, e, zs, zr, zx, zq, edges):
    first, nx, ny, nz, rows, hy = lev.first, lev.nx, lev.ny, lev.nz, lev.rows, lev.hy
    every, lanes = pl.ds(0, 3), pl.ds(0, nz)

    def planes(dx, skip, w):
        if dx == 0:
            return pl.ds(first, nx), pl.ds(first, nx)
        if dx > 0:
            return pl.ds(first + nx - skip - w, w), pl.ds(first - skip - w, w)
        return pl.ds(first + skip, w), pl.ds(first + nx + skip, w)

    def lines(dy, skip=0, w=hy):
        if dy == 0:
            return pl.ds(0, ny), pl.ds(0, ny)
        if dy > 0:
            return pl.ds(ny - skip - w, w), pl.ds(rows - skip - w, w)
        return pl.ds(skip, w), pl.ds(ny + skip, w)

    def flat(dx, dy, arrays, x_part, y_part=(0, hy)):
        xs, xd = planes(dx, *x_part)
        ys, yd = lines(dy, *y_part)
        return e.at[arrays, xs, ys, lanes], e.at[arrays, xd, yd, lanes], (dx, dy, 0)

    found = {key: [] for key in ("x", "y", "z", "xy", "xz", "yz", "xyz", "far")}
    for dx in (1, -1):
        for a, (whole, w) in enumerate(zip(inputs, (3, 2, 2))):
            xd = planes(dx, 0, w)[1]
            source = whole.at[pl.ds(nx - w if dx > 0 else 0, w)]
            found["x"].append((source, e.at[a, xd, pl.ds(0, ny), lanes], (dx, 0, 0)))
    for dx in (1, -1):
        for dy in (1, -1):
            found["xy"].append(flat(dx, dy, every, (0, 2), (0, 2)))
    for dz in (1, -1):
        side = 1 if dz > 0 else 0
        for dx in (1, -1):
            for dy in (0, 1, -1):
                ys, yd = lines(dy)
                xside = 1 if dx > 0 else 0
                found["xyz" if dy else "xz"].append((zx.at[side, xside, ys], zq.at[1 - side, 1 - xside, yd], (dx, dy, dz)))
    for dy in (1, -1):
        found["y"].append(flat(0, dy, every, (0, nx)))
    for dz in (1, -1):
        side = 1 if dz > 0 else 0
        for dy in (0, 1, -1):
            ys, yd = lines(dy)
            found["yz" if dy else "z"].append((zs.at[side, :, ys], zr.at[1 - side, :, yd], (0, dy, dz)))
    for dx in (1, -1):
        found["far"].append(flat(dx, 0, pl.ds(0, 1), (3, 2)))
        found["far"].append(flat(dx, 0, pl.ds(1, 2), (2, 2)))
        for dy in (1, -1):
            xs, ys = planes(dx, 0, 5)[0], lines(dy)[0]
            low = 1 if dy > 0 else 0
            place = (2 if dx < 0 else 0) + low
            found["far"].append((e.at[every, xs, ys, lanes], edges.at[place, :, :, pl.ds(3 * low, hy)], (dx, dy, 0)))
    return found


def halo_messages(lev, a_first, a_count, widths, e, zs, zr):
    first, nx, ny, rows, hy = lev.first, lev.nx, lev.ny, lev.rows, lev.hy

    def planes(dx, w):
        if dx == 0:
            return pl.ds(first, nx), pl.ds(first, nx)
        if dx > 0:
            return pl.ds(first + nx - w, w), pl.ds(first - w, w)
        return pl.ds(first, w), pl.ds(first + nx, w)

    def lines(dy):
        if dy == 0:
            return pl.ds(0, ny), pl.ds(0, ny)
        if dy > 0:
            return pl.ds(ny - hy, hy), pl.ds(rows - hy, hy)
        return pl.ds(0, hy), pl.ds(ny, hy)

    found = []
    for dz in (0, -1, 1):
        for dx in (1, -1, 0):
            for dy in (0, 1, -1):
                if dx == dy == dz == 0:
                    continue
                ys, yd = lines(dy)
                if dz == 0:
                    groups = [(a_first, a_count, max(widths))]
                    if dy == 0 and len(widths) > 1:
                        groups = []
                        a = a_first
                        for w, n in ((widths[0], 1), (widths[1], a_count - 1)):
                            groups.append((a, n, w))
                            a += n
                    for a, n, w in groups:
                        xs, xd = planes(dx, w)
                        found.append(
                            (
                                e.at[pl.ds(a, n), xs, ys, pl.ds(0, lev.nz)],
                                e.at[pl.ds(a, n), xd, yd, pl.ds(0, lev.nz)],
                                (dx, dy, dz),
                            )
                        )
                else:
                    side = 1 if dz > 0 else 0
                    slot = 1 - dx
                    found.append(
                        (zs.at[side, :, ys], zr.at[1 - side, slot, :, yd], (dx, dy, dz))
                    )
    return found


GATHER = [
    (dx, 0, dz) for dx in (1, 3, 2, 0) for dz in (0, 1, -1) if (dx, dz) != (0, 0)
]
NEAR = [
    (dx, dy, dz)
    for dx in (-1, 0, 1)
    for dy in (-1, 0, 1)
    for dz in (-1, 0, 1)
    if (dx, dy, dz) != (0, 0, 0)
]
MESSAGES = 30 + 8 + 26 + 26 + 11 + 6 + 11 + 4


def kernel(
    sizes, rhs, cond, absb, fx0, fy0, fz0, inv0, diag0, src0, v0, u0,
    e0, mask0, miss0, zs0, zr0, zx0, zq0, edges0,
    e1, fx1, fy1, fz1, inv1, diag1, src1, v1, u1, mask1, miss1, zs1, zr1, zt1, zu1,
    e2, fx2, fy2, fz2, inv2, diag2, src2, v2, u2, mask2, miss2, own2, cut2, gatc, gats, gatz,
    e3, fx3, fy3, fz3, inv3, diag3, src3, v3, u3, mask3, miss3,
    p01, p12, p23, s32, s21, s10, tmp, send, recv, local, met,
):
    gx, gy, gz = (lax.axis_index(axis) for axis in AXES)
    own0 = (pl.ds(L0.first, L0.nx), pl.ds(0, L0.ny), pl.ds(0, L0.nz))
    loads = [
        pltpu.make_async_copy(source, e0.at[(a,) + own0], local.at[a])
        for a, source in enumerate((cond, absb, rhs))
    ]
    for copy in loads:
        copy.start()

    barrier = pltpu.get_barrier_semaphore()
    faces = [partner(offset, sizes) for offset in NEAR if sum(map(abs, offset)) == 1]

    def greet(semaphore):
        for device in faces:
            pl.semaphore_signal(semaphore, inc=1, device_id=device, device_id_type=MESH)

    greet(barrier)
    started = []

    def post(messages):
        copies = []
        for source, target, offset in messages:
            k = len(started)
            copy = pltpu.make_async_remote_copy(
                src_ref=source,
                dst_ref=target,
                send_sem=send.at[k],
                recv_sem=recv.at[k],
                device_id=partner(offset, sizes),
                device_id_type=MESH,
            )
            copy.start()
            started.append(copy)
            copies.append(copy)
        return copies

    def arrive(copies):
        for copy in copies:
            copy.wait_recv()

    def gather_a(arrays, gat):
        lane = iota((L2.ny, 128), 1)
        group = lax.shift_right_logical(lane, 5)
        for a in arrays:
            low = high = jnp.zeros((L2.ny, 128), F32)
            for q in range(4):
                plane = own2[a, q]
                low = jnp.where(group == q, pltpu.roll(plane, 32 * q, 1) if q else plane, low)
                high = jnp.where(group == q, pltpu.roll(plane, 32 * q - 32, 1) if q > 1 else (plane if q else pltpu.roll(plane, 96, 1)), high)
            cut2[0, a] = low
            cut2[1, a] = high
        if len(arrays) == 2:
            for q in range(4):
                own2[3, q] = jnp.where(lane < 64, own2[0, q], pltpu.roll(own2[1, q], 64, 1))
        whole = 3 if len(arrays) == 2 else arrays[0]
        first = pl.ds(arrays[0], len(arrays))
        mine = pl.ds(L2.nx * gx, L2.nx)
        gat[mine] = own2[whole]
        messages = []
        for dx, dy, dz in GATHER:
            if dz == 0:
                messages.append((own2.at[whole], gat.at[mine], (dx, dy, dz)))
            else:
                side = 1 if dz > 0 else 0
                messages.append((cut2.at[side, first], gatz.at[side, gx, first], (dx, dy, dz)))
        return messages

    def combine(a, gat):
        lane = iota((L2.ny, 128), 1)
        for p in range(16):
            q = p % 4
            far = pltpu.roll(gatz[0, p // 4, a], (64 - 32 * q) % 128, 1) if q != 2 else gatz[0, p // 4, a]
            low = pltpu.roll(gatz[1, p // 4, a], (96 - 32 * q) % 128, 1) if q != 3 else gatz[1, p // 4, a]
            mine = pltpu.roll(gat[p], 64, 1) if a == 1 else gat[p]
            e2[a, L2.first + p, pl.ds(0, 8)] = jnp.where(lane < 64, mine, jnp.where(lane < 96, far, low))

    def gather_b(a, n):
        x = pl.ds(L2.first, 16)
        mine = e2.at[pl.ds(a, n), x, pl.ds(0, 8)]
        messages = [
            (mine, e2.at[pl.ds(a, n), x, pl.ds(row, 8)], (0, dy, 0))
            for dy, row in ((1, 40), (-1, 8), (2, 32), (-2, 16))
        ]
        if a == 0:
            for dy, row, to in ((3, 7, 31), (-3, 0, 24)):
                messages.append(
                    (e2.at[pl.ds(0, 1), x, pl.ds(row, 1)], e2.at[pl.ds(0, 1), x, pl.ds(to, 1)], (0, dy, 0))
                )
        return messages

    messages = fine_messages(L0, (cond, absb, rhs), e0, zs0, zr0, zx0, zq0, edges0)
    pl.semaphore_wait(barrier, 6)
    round_1x = post(messages["x"])
    greet(met.at[0])
    for copy in loads:
        copy.wait()
    round_1 = post(messages["y"])
    pack(L0, 3, 0, e0, zs0)
    pack_edges(L0, zs0, zx0)
    round_1 += post(messages["z"])
    pl.semaphore_wait(met.at[0], 6)
    greet(met.at[1])
    round_1x += post(messages["xy"]) + post(messages["xz"])
    round_1 += post(messages["yz"])
    pl.semaphore_wait(met.at[1], 6)
    round_1x += post(messages["xyz"])
    for lev, mask, miss in ((L0, mask0, miss0), (L1, mask1, miss1), (L2, mask2, miss2), (L3, mask3, miss3)):
        make_mask(lev, sizes, mask, miss)
    p01[...] = pool_matrix(L0, L1)[:256, :128]
    p12[...] = pool_matrix(L1, L2)[:128]
    p23[...] = pool_matrix(L2, L3)
    s32[...] = spread_matrix(L3, L2)
    s21[...] = spread_matrix(L2, L1)
    s10[...] = spread_matrix(L1, L0)
    for p in (0, 1, 18, 19):
        for ref in (e2.at[0], v2, u2):
            ref[p] = jnp.zeros((L2.rows, L2.lanes), F32)
    e2[1, pl.ds(2, 16), pl.ds(24, 8)] = jnp.ones((16, 8, 128), F32)
    e2[2, pl.ds(2, 16), pl.ds(24, 8)] = jnp.zeros((16, 8, 128), F32)
    for p in (0, 9):
        for ref in (e3.at[0], v3, u3):
            ref[p] = jnp.zeros((L3.rows, L3.lanes), F32)

    for a in range(2):

        def stage1(p0, n, a=a):
            for k in range(n):
                q = p0 + k
                p = L0.first + 2 * q
                rows, lanes = pl.ds(0, 32), pl.ds(0, 256)
                stage(tmp, q, e0[a, p, rows, lanes] + e0[a, p + 1, rows, lanes])

        blocks(0, 8, 4, stage1)
        for q, plane in enumerate(pool(tmp, 8, 32, 2, p01)):
            e1[a, L1.first + q, pl.ds(0, 16), pl.ds(0, 128)] = plane
    for a in range(2):
        for q in range(4):
            p = L1.first + 2 * q
            rows, lanes = pl.ds(0, 16), pl.ds(0, 128)
            stage(tmp, 4 * a + q, e1[a, p, rows, lanes] + e1[a, p + 1, rows, lanes])
    for q, plane in enumerate(pool(tmp, 8, 16, 1, p12)):
        own2[q // 4, q % 4] = plane
    round_c2 = post(gather_a((0, 1), gatc))
    pack(L1, 2, 0, e1, zs1)
    round_c1 = post(halo_messages(L1, 0, 2, (6,), e1, zs1, zr1))

    base0 = L0.nx * gx - L0.first
    level0 = (fx0, fy0, fz0, inv0)
    arrive(round_1)
    unpack_own(L0, e0, zr0)

    def build0(lo, hi, step=2):
        build(L0, base0, 64, lo, hi, step, e0, mask0, miss0, *level0, diag0, src0, v0, W[0])

    build0(6, 20)
    sweep(7, 19, 2, src0, *level0, v0, u0, W[1])
    arrive(round_1x)
    unpack_edges(L0, e0, zq0)
    build0(3, 6, 3)
    build0(20, 23, 3)
    sweep(4, 7, 3, src0, *level0, v0, u0, W[1])
    sweep(19, 22, 3, src0, *level0, v0, u0, W[1])

    def res0(p):
        return remainder(L0.first + p, src0, fx0, fy0, fz0, diag0, u0)[:32, :256]

    def stage_s1(p0, n):
        for k in range(n):
            q = p0 + k
            stage(tmp, q, res0(2 * q) + res0(2 * q + 1))

    blocks(0, 8, 1, stage_s1)
    for q, plane in enumerate(pool(tmp, 8, 32, 2, p01)):
        e1[2, L1.first + q, pl.ds(0, 16), pl.ds(0, 128)] = plane
    pack(L1, 1, 2, e1, zt1)
    round_2 = post(halo_messages(L1, 2, 1, (5,), e1, zt1, zu1))

    arrive(round_c2)
    combine(0, gatc)
    combine(1, gatc)
    round_d2 = post(gather_b(0, 2))
    base1 = L1.nx * gx - L1.first
    level1 = (fx1, fy1, fz1, inv1)
    arrive(round_c1)
    unpack(L1, 2, 0, e1, zr1)
    build(L1, base1, 32, 1, 19, 3, e1, mask1, miss1, *level1, diag1, src1, v1, None)

    arrive(round_2)
    unpack(L1, 1, 2, e1, zu1)
    first_sweep(L1, base1, 32, 1, 19, 6, e1, mask1, inv1, src1, v1, W[0])
    sweep(2, 18, 4, src1, *level1, v1, u1, W[1])

    def res1(p):
        return remainder(L1.first + p, src1, fx1, fy1, fz1, diag1, u1)[:16, :128]

    for q in range(4):
        stage(tmp, q, res1(2 * q) + res1(2 * q + 1))
    for q, plane in enumerate(pool(tmp, 4, 16, 1, p12)):
        own2[2, q] = plane
    round_3 = post(gather_a((2,), gats))
    round_f = post(messages["far"])

    arrive(round_d2)
    level2 = (fx2, fy2, fz2, inv2)
    level3 = (fx3, fy3, fz3, inv3)
    build(L2, -L2.first, 16, 2, 18, 4, e2, mask2, miss2, *level2, diag2, src2, v2, None)
    for a in range(2):
        for q in range(8):
            stage(tmp, q, e2[a, L2.first + 2 * q] + e2[a, L2.first + 2 * q + 1])
        for q, plane in enumerate(pool(tmp, 8, 48, 1, p23)):
            e3[a, L3.first + q] = plane
    build(L3, -L3.first, 8, 1, 9, 8, e3, mask3, miss3, *level3, diag3, src3, v3, None)

    arrive(round_3)
    combine(2, gats)
    round_4 = post(gather_b(2, 1))

    arrive(round_f)
    for place in range(4):
        for k in range(5):
            p = k if place < 2 else 21 + k
            for a in range(3):
                e0[a, p, pl.ds(40 if place % 2 else 32, 8), pl.ds(0, 256)] = edges0[place, a, k]
    build0(1, 6, 5)
    build0(20, 25, 5)
    sweep(2, 7, 5, src0, *level0, v0, u0, W[1])
    sweep(19, 24, 5, src0, *level0, v0, u0, W[1])
    arrive(round_4)

    first_sweep(L2, -L2.first, 16, 2, 18, 8, e2, mask2, inv2, src2, v2, W[0])
    sweep(2, 18, 4, src2, *level2, v2, u2, W[1])

    def stage_s3(p0, n):
        for k in range(n):
            q = p0 + k
            pair = [remainder(L2.first + 2 * q + j, src2, fx2, fy2, fz2, diag2, u2) for j in (0, 1)]
            stage(tmp, q, pair[0] + pair[1])

    blocks(0, 8, 2, stage_s3)
    for q, plane in enumerate(pool(tmp, 8, 48, 1, p23)):
        e3[2, L3.first + q] = plane
    first_sweep(L3, -L3.first, 8, 1, 9, 8, e3, mask3, inv3, src3, v3, W6[0])
    here, there = v3, u3
    for weight in W6[1:]:
        sweep(1, 9, 8, src3, *level3, here, there, weight)
        here, there = there, here

    spread([here[L3.first + q] for q in range(8)], tmp, s32, 24, 0)
    for q in range(8):
        plane = staged(tmp, q, 48, 1)
        for k in (0, 1):
            u2[L2.first + 2 * q + k] += plane
    sweep(2, 18, 4, src2, *level2, u2, v2, W[0])
    sweep(2, 18, 4, src2, *level2, v2, u2, W[1])

    wide = [u2[L2.nx * gx + q] for q in range(8)]
    wide = [jnp.concatenate([plane[:16], plane[40:]], axis=0) for plane in wide]
    spread(wide, tmp, s21, 16, 4)

    def add1(q0, n):
        for j in range(n):
            plane = staged(tmp, q0 + j, 32, 2)
            for k in (0, 1):
                u1[L1.first - 4 + 2 * (q0 + j) + k] += plane

    blocks(0, 8, 2, add1)
    sweep(3, 17, 7, src1, *level1, u1, v1, W[0])
    sweep(4, 16, 6, src1, *level1, v1, u1, W[1])

    spread([u1[L1.first - 2 + q] for q in range(12)], tmp, s10, 24, 4)

    def add0(q0, n):
        for j in range(n):
            plane = staged(tmp, q0 + j, 48, 3)
            for k in (0, 1):
                u0[L0.first - 4 + 2 * (q0 + j) + k] += plane

    blocks(0, 12, 2, add0)
    sweep(3, 23, 2, src0, *level0, u0, v0, W[0])
    for copy in started:
        copy.wait_send()


def finish(fx0, fy0, fz0, inv0, diag0, src0, v0, sol_out, res_out, u0, res, done):
    level0 = (fx0, fy0, fz0, inv0)
    copies = []

    def send(source, target):
        copies.append(pltpu.make_async_copy(source, target, done.at[len(copies)]))
        copies[-1].start()

    own = pl.ds(0, 32), pl.ds(0, 256)
    first = L0.first
    sweep(first - 1, first + 1, 2, src0, *level0, v0, u0, W[1])
    for p in range(0, 16, 4):
        lo = p + 1
        sweep(first + lo, first + lo + 4, 4, src0, *level0, v0, u0, W[1])
        send(u0.at[(pl.ds(first + p, 4),) + own], sol_out.at[pl.ds(p, 4)])
    for p in range(0, 16, 4):
        for k in range(p, p + 4):
            res[k] = remainder(first + k, src0, fx0, fy0, fz0, diag0, u0)[:32, :256]
        send(res.at[pl.ds(p, 4)], res_out.at[pl.ds(p, 4)])
    for copy in copies:
        copy.wait()


def solution(mesh):
    sizes = tuple(mesh.shape[axis] for axis in AXES)

    def vmem(*shape):
        return pltpu.VMEM(shape, F32)

    def level(lev):
        return [vmem(3, *lev.shape)] + [vmem(*lev.shape)] * 8 + [vmem(lev.rows, lev.lanes)] * 2

    scratch = [
        vmem(3, *L0.shape), vmem(L0.rows, L0.lanes), vmem(L0.rows, L0.lanes), vmem(2, 3, 32, 128), vmem(2, 3, 48, 128), vmem(2, 2, 32, 128), vmem(2, 2, 48, 128), vmem(4, 3, 5, 8, 256),
        *level(L1), vmem(2, 2, 16, 128), vmem(2, 3, 2, 32, 128), vmem(2, 1, 16, 128), vmem(2, 3, 1, 32, 128),
        *level(L2), vmem(4, 4, 8, 128), vmem(2, 3, 8, 128), vmem(16, 8, 128), vmem(16, 8, 128), vmem(2, 4, 3, 8, 128),
        *level(L3),
        vmem(256, 128), vmem(128, 128), vmem(128, 128), vmem(128, 128), vmem(128, 256), vmem(256, 384),
        vmem(12, 3, 48, 128),
        pltpu.SemaphoreType.DMA((MESSAGES,)),
        pltpu.SemaphoreType.DMA((MESSAGES,)),
        pltpu.SemaphoreType.DMA((3,)),
        pltpu.SemaphoreType.REGULAR((2,)),
    ]

    def cycle(right_side, conductivity, absorption):
        block = jax.ShapeDtypeStruct((16, 32, 256), F32)
        inner = pl.BlockSpec(memory_space=pltpu.VMEM)
        outer = pl.BlockSpec(memory_space=pltpu.HBM)
        fine = pl.pallas_call(
            functools.partial(kernel, sizes),
            out_shape=(vmem(*L0.shape),) * 8,
            in_specs=[outer] * 3,
            out_specs=(inner,) * 8,
            scratch_shapes=scratch,
            compiler_params=pltpu.CompilerParams(
                collective_id=0, has_side_effects=True, vmem_limit_bytes=49 * 2**20
            ),
        )(right_side, conductivity, absorption)
        return pl.pallas_call(
            finish,
            out_shape=(block, block),
            in_specs=[inner] * 7,
            out_specs=(outer, outer),
            scratch_shapes=[
                vmem(*L0.shape),
                vmem(*block.shape),
                pltpu.SemaphoreType.DMA((8,)),
            ],
            compiler_params=pltpu.CompilerParams(vmem_limit_bytes=12 * 2**20),
        )(*fine[:7])

    placed = P(*AXES)
    return jax.shard_map(
        cycle, mesh=mesh, in_specs=(placed,) * 3, out_specs=(placed, placed), check_vma=False
    )
```

```python
import functools
import math

import jax
import jax.numpy as jnp
from jax import lax
from jax.experimental import pallas as pl
from jax.experimental.pallas import tpu as pltpu
from jax.sharding import PartitionSpec as P

MESH = pl.DeviceIdType.MESH
AXES = ("gx", "gy", "gz")
EIGEN_LOW = 0.25
EIGEN_HIGH = 2.0
F32 = jnp.float32


def chebyshev_weights(count):
    middle = 0.5 * (EIGEN_HIGH + EIGEN_LOW)
    radius = 0.5 * (EIGEN_HIGH - EIGEN_LOW)
    return [
        1.0 / (middle + radius * math.cos(math.pi * (2 * step + 1) / (2 * count)))
        for step in range(count)
    ]


W = chebyshev_weights(2)
W6 = chebyshev_weights(6)


GATHER = [
    (dx, 0, dz) for dx in (1, 3, 2, 0) for dz in (0, 1, -1) if (dx, dz) != (0, 0)
]
NEAR = [
    (dx, dy, dz)
    for dx in (-1, 0, 1)
    for dy in (-1, 0, 1)
    for dz in (-1, 0, 1)
    if (dx, dy, dz) != (0, 0, 0)
]


class Level:
    def __init__(self, scale, own, planes, first, rows, lanes, reach):
        self.scale = scale
        self.nx, self.ny, self.nz = own
        self.planes, self.first = planes, first
        self.rows, self.lanes = rows, lanes
        self.hy, self.hz = reach

    @property
    def shape(self):
        return (self.planes, self.rows, self.lanes)


L0 = Level(1.0, (16, 32, 256), 26, 5, 48, 384, (5, 8))
L1 = Level(0.25, (8, 16, 128), 20, 6, 32, 256, (6, 8))
L2 = Level(0.25**2, (4, 8, 64), 20, 2, 48, 128, (17, 32))
L3 = Level(0.25**3, (2, 4, 32), 10, 1, 24, 128, (8, 16))


def partner(offset, sizes):
    place = []
    for axis, step, size in zip(AXES, offset, sizes):
        index = lax.axis_index(axis)
        place.append(index if step == 0 else lax.rem(index + (step + size), size))
    return tuple(place)


def up(value, axis):
    return pltpu.roll(value, value.shape[axis] - 1, axis)


def down(value, axis):
    return pltpu.roll(value, 1, axis)


def iota(shape, axis):
    return lax.broadcasted_iota(jnp.int32, shape, axis)


def make_mask(lev, sizes, mask_ref, miss_ref):
    shape = (lev.rows, lev.lanes)
    gy, gz = lax.axis_index("gy"), lax.axis_index("gz")
    row, lane = iota(shape, 0), iota(shape, 1)
    y = jnp.where(row < lev.ny + lev.hy, row, row - lev.rows)
    z = jnp.where(lane < lev.nz + lev.hz, lane, lane - lev.lanes)
    yy, zz = y + gy * lev.ny, z + gz * lev.nz
    ymax, zmax = lev.ny * sizes[1], lev.nz * sizes[2]
    good = (y >= -lev.hy) & (z >= -lev.hz) & (yy >= 0) & (yy < ymax) & (zz >= 0) & (zz < zmax)
    mask_ref[...] = jnp.where(good, 1.0, 0.0)
    miss = jnp.where(yy == 0, 1.0, 0.0) + jnp.where(yy == ymax - 1, 1.0, 0.0)
    miss_ref[...] = miss + jnp.where(zz == 0, 1.0, 0.0) + jnp.where(zz == zmax - 1, 1.0, 0.0)


def blocks(lo, hi, step, body):
    full = (hi - lo) // step

    def one(i, carry):
        body(lo + i * step, step)
        return carry

    if full == 1:
        body(lo, step)
    elif full:
        lax.fori_loop(0, full, one, 0)
    if (hi - lo) % step:
        body(lo + full * step, (hi - lo) % step)


def inside(p, base, xmax, mask_ref):
    x = p + base
    return mask_ref[...] > jnp.where((x >= 0) & (x < xmax), 0.5, 2.0)


def build(lev, base, xmax, lo, hi, step, e, mask_ref, miss_ref, fx, fy, fz, inv, diag, src, v, weight):
    scale = lev.scale

    def face(a, b):
        return jnp.where(jnp.minimum(a, b) > 0.0, (0.5 * scale) * (a + b), 0.0)

    def masked(p):
        return jnp.where(inside(p, base, xmax, mask_ref), e[0, p], 0.0)

    fx[lo - 1] = face(masked(lo - 1), masked(lo))

    def body(p0, n):
        cur = masked(p0)
        fxm = fx[p0 - 1]
        for k in range(n):
            p = p0 + k
            x = p + base
            after = masked(p + 1)
            fxp = face(cur, after)
            fx[p] = fxp
            fyp = face(cur, up(cur, 0))
            fy[p] = fyp
            fzp = face(cur, up(cur, 1))
            fz[p] = fzp
            edge = jnp.where(x == 0, 1.0, 0.0) + jnp.where(x == xmax - 1, 1.0, 0.0)
            total = (fxm + fxp) + (fyp + down(fyp, 0)) + (fzp + down(fzp, 1))
            total = total + (scale * cur) * (miss_ref[...] + edge)
            mine = inside(p, base, xmax, mask_ref)
            d = e[1, p] + total
            diag[p] = jnp.where(mine, d, 0.0)
            i = jnp.where(mine, 1.0 / d, 0.0)
            inv[p] = i
            if weight is not None:
                s = jnp.where(mine, e[2, p], 0.0)
                src[p] = s
                v[p] = weight * i * s
            cur, fxm = after, fxp

    blocks(lo, hi, step, body)


def first_sweep(lev, base, xmax, lo, hi, step, source, mask_ref, inv, src, v, weight):
    def body(p0, n):
        for k in range(n):
            p = p0 + k
            s = jnp.where(inside(p, base, xmax, mask_ref), source[p], 0.0)
            src[p] = s
            v[p] = weight * inv[p] * s

    blocks(lo, hi, step, body)


def flow(p, v, fx, fy, fz):
    cur = v[p]
    fyp, fzp = fy[p], fz[p]
    total = fx[p] * v[p + 1] + fx[p - 1] * v[p - 1]
    total = total + (fyp * up(cur, 0) + down(fyp * cur, 0))
    return cur, total + (fzp * up(cur, 1) + down(fzp * cur, 1))


def sweep(lo, hi, step, src, fx, fy, fz, inv, v, out, weight):
    def body(p0, n):
        for k in range(n):
            p = p0 + k
            cur, total = flow(p, v, fx, fy, fz)
            out[p] = (1.0 - weight) * cur + (weight * inv[p]) * (src[p] + total)

    blocks(lo, hi, step, body)


def remainder(p, src, fx, fy, fz, diag, v):
    cur, total = flow(p, v, fx, fy, fz)
    return (src[p] - diag[p] * cur) + total


def pool_matrix(fine, coarse):
    shape = (fine.lanes, coarse.lanes)
    f, c = iota(shape, 0), iota(shape, 1)
    zf = jnp.where(f < fine.nz + fine.hz, f, f - fine.lanes)
    zc = jnp.where(c < coarse.nz + coarse.hz, c, c - coarse.lanes)
    hit = (zf >= 2 * zc) & (zf < 2 * zc + 2) & (zc >= -coarse.hz)
    return jnp.where(hit, 0.125, 0.0)


def spread_matrix(coarse, fine):
    shape = (coarse.lanes, fine.lanes)
    c, f = iota(shape, 0), iota(shape, 1)
    zf = jnp.where(f < fine.nz + fine.hz, f, f - fine.lanes)
    zc = jnp.where(c < coarse.nz + coarse.hz, c, c - coarse.lanes)
    hit = (zf >= 2 * zc) & (zf < 2 * zc + 2) & (zf >= -fine.hz)
    return jnp.where(hit, 1.0, 0.0)


def dot(a, b):
    high = a.astype(jnp.bfloat16)
    low = (a - high.astype(F32)).astype(jnp.bfloat16)
    b = b.astype(jnp.bfloat16)
    return jnp.dot(high, b, preferred_element_type=F32) + jnp.dot(low, b, preferred_element_type=F32)


def stage(tmp, q, plane):
    rows, lanes = plane.shape
    for k in range(lanes // 128):
        tmp[q, k, pl.ds(0, rows)] = plane[:, 128 * k : 128 * (k + 1)]


def pool(tmp, count, rows, tiles, matrix):
    parts = []
    for k in range(tiles):
        lines = []
        for q in range(count):
            even = tmp[q, k, pl.ds(0, rows // 2, stride=2)]
            odd = tmp[q, k, pl.ds(1, rows // 2, stride=2)]
            lines.append(even + odd)
        parts.append(jnp.concatenate(lines, axis=0))
    both = parts[0] if tiles == 1 else jnp.concatenate(parts, axis=1)
    done = dot(both, matrix[...])
    return [done[q * (rows // 2) : (q + 1) * (rows // 2)] for q in range(count)]


def spread(planes, tmp, matrix, rows, wrap):
    size = planes[0].shape[0]
    wide = dot(jnp.concatenate(planes, axis=0), matrix[...])
    for q in range(len(planes)):
        for k in range(wide.shape[1] // 128):
            part = wide[q * size : (q + 1) * size, 128 * k : 128 * (k + 1)]
            for odd in (0, 1):
                tmp[q, k, pl.ds(odd, rows - wrap, stride=2)] = part[: rows - wrap]
                if wrap:
                    tmp[q, k, pl.ds(2 * (rows - wrap) + odd, wrap, stride=2)] = part[size - wrap :]


def staged(tmp, q, rows, tiles):
    parts = [tmp[q, k, pl.ds(0, rows)] for k in range(tiles)]
    return parts[0] if tiles == 1 else jnp.concatenate(parts, axis=1)


def pack(lev, a_count, a_first, e, zs):
    shape = (lev.ny, 128)
    group = lax.shift_right_logical(iota(shape, 1), 3)
    for a in range(a_count):
        low = high = jnp.zeros(shape, F32)
        for x in range(lev.nx):
            p = lev.first + x
            lows = e[a_first + a, p, pl.ds(0, lev.ny), pl.ds(0, 128)]
            highs = e[a_first + a, p, pl.ds(0, lev.ny), pl.ds(lev.nz - 128, 128)]
            if x:
                lows = pltpu.roll(lows, 8 * x, 1)
            if x < 15:
                highs = pltpu.roll(highs, 8 * x + 8, 1)
            low = jnp.where(group == x, lows, low)
            high = jnp.where(group == x, highs, high)
        zs[0, a] = low
        zs[1, a] = high


def pack_edges(lev, zs, zx):
    shape = (lev.ny, 128)
    lane = iota(shape, 1)
    width = 8 * lev.first
    for side in (0, 1):
        for xside in (0, 1):
            total = jnp.zeros(shape, F32)
            for a in range(3):
                shift = width * a - (0 if xside == 0 else 128 - width)
                part = zs[side, a]
                if shift % 128:
                    part = pltpu.roll(part, shift % 128, 1)
                total = jnp.where((lane >= width * a) & (lane < width * (a + 1)), part, total)
            zx[side, xside] = total


def unpack_own(lev, e, zr):
    lane = iota((lev.rows, 128), 1)

    def body(x0, n):
        for k in range(n):
            x = x0 + k
            for a in range(3):
                low = pltpu.roll(zr[0, a], 120 - 8 * x, 1)
                high = pltpu.roll(zr[1, a], lax.rem(128 - 8 * x, 128), 1)
                e[a, lev.first + x, :, pl.ds(lev.nz, 128)] = jnp.where(lane < 64, high, low)

    blocks(0, lev.nx, 4, body)


def unpack_edges(lev, e, zq):
    lane = iota((lev.rows, 128), 1)
    for slot in (0, 1):
        for a in range(3):
            for k in range(lev.first):
                x = a * lev.first + k
                p = k if slot == 0 else lev.first + lev.nx + k
                low = pltpu.roll(zq[0, slot], 120 - 8 * x, 1) if x < 15 else zq[0, slot]
                high = pltpu.roll(zq[1, slot], 128 - 8 * x, 1) if x else zq[1, slot]
                e[a, p, :, pl.ds(lev.nz, 128)] = jnp.where(lane < 64, high, low)


def unpack(lev, a_count, a_first, e, zr):
    lane = iota((lev.rows, 128), 1)
    spans = ((0, 0, lev.first), (1, lev.first, lev.nx), (2, lev.first + lev.nx, lev.first))
    for slot, start, count in spans:
        offset = lev.nx - lev.first if slot == 0 else 0
        for k in range(count):
            x = k + offset
            for a in range(a_count):
                low = pltpu.roll(zr[0, slot, a], 120 - 8 * x, 1)
                high = zr[1, slot, a]
                if x:
                    high = pltpu.roll(high, 128 - 8 * x, 1)
                e[a_first + a, start + k, :, pl.ds(lev.nz, 128)] = jnp.where(lane < 64, high, low)


def fine_messages(lev, inputs, e, zs, zr, zx, zq, edges):
    first, nx, ny, nz, rows, hy = lev.first, lev.nx, lev.ny, lev.nz, lev.rows, lev.hy
    every, lanes = pl.ds(0, 3), pl.ds(0, nz)

    def planes(dx, skip, w):
        if dx == 0:
            return pl.ds(first, nx), pl.ds(first, nx)
        if dx > 0:
            return pl.ds(first + nx - skip - w, w), pl.ds(first - skip - w, w)
        return pl.ds(first + skip, w), pl.ds(first + nx + skip, w)

    def lines(dy, skip=0, w=hy):
        if dy == 0:
            return pl.ds(0, ny), pl.ds(0, ny)
        if dy > 0:
            return pl.ds(ny - skip - w, w), pl.ds(rows - skip - w, w)
        return pl.ds(skip, w), pl.ds(ny + skip, w)

    def flat(dx, dy, arrays, x_part, y_part=(0, hy)):
        xs, xd = planes(dx, *x_part)
        ys, yd = lines(dy, *y_part)
        return e.at[arrays, xs, ys, lanes], e.at[arrays, xd, yd, lanes], (dx, dy, 0)

    found = {key: [] for key in ("x", "y", "z", "xy", "xz", "yz", "xyz", "far")}
    for dx in (1, -1):
        for a, (whole, w) in enumerate(zip(inputs, (3, 2, 2))):
            xd = planes(dx, 0, w)[1]
            source = whole.at[pl.ds(nx - w if dx > 0 else 0, w)]
            found["x"].append((source, e.at[a, xd, pl.ds(0, ny), lanes], (dx, 0, 0)))
    for dx in (1, -1):
        for dy in (1, -1):
            found["xy"].append(flat(dx, dy, every, (0, 2), (0, 2)))
    for dz in (1, -1):
        side = 1 if dz > 0 else 0
        for dx in (1, -1):
            for dy in (0, 1, -1):
                ys, yd = lines(dy)
                xside = 1 if dx > 0 else 0
                found["xyz" if dy else "xz"].append((zx.at[side, xside, ys], zq.at[1 - side, 1 - xside, yd], (dx, dy, dz)))
    for dy in (1, -1):
        found["y"].append(flat(0, dy, every, (0, nx)))
    for dz in (1, -1):
        side = 1 if dz > 0 else 0
        for dy in (0, 1, -1):
            ys, yd = lines(dy)
            found["yz" if dy else "z"].append((zs.at[side, :, ys], zr.at[1 - side, :, yd], (0, dy, dz)))
    for dx in (1, -1):
        found["far"].append(flat(dx, 0, pl.ds(0, 1), (3, 2)))
        found["far"].append(flat(dx, 0, pl.ds(1, 2), (2, 2)))
        for dy in (1, -1):
            xs, ys = planes(dx, 0, 4)[0], lines(dy, 0, 4)[0]
            low = 1 if dy > 0 else 0
            place = (2 if dx < 0 else 0) + low
            found["far"].append((e.at[every, xs, ys, lanes], edges.at[place, :, :, pl.ds(4 * low, 4)], (dx, dy, 0)))
    return found


def halo_messages(lev, a_first, a_count, width, hy, axes, e, zs, zr):
    first, nx, ny, rows = lev.first, lev.nx, lev.ny, lev.rows
    arrays, lanes = pl.ds(a_first, a_count), pl.ds(0, lev.nz)

    def planes(dx):
        if dx == 0:
            return pl.ds(first, nx), pl.ds(first, nx)
        if dx > 0:
            return pl.ds(first + nx - width, width), pl.ds(first - width, width)
        return pl.ds(first, width), pl.ds(first + nx, width)

    def lines(dy):
        if dy == 0:
            return pl.ds(0, ny), pl.ds(0, ny)
        if dy > 0:
            return pl.ds(ny - hy, hy), pl.ds(rows - hy, hy)
        return pl.ds(0, hy), pl.ds(ny, hy)

    found = []
    for dx, dy, dz in sorted(NEAR, key=lambda offset: -sum(map(abs, offset))):
        if abs(dx) + abs(dy) + abs(dz) > axes:
            continue
        xs, xd = planes(dx)
        ys, yd = lines(dy)
        if dz == 0:
            pair = e.at[arrays, xs, ys, lanes], e.at[arrays, xd, yd, lanes]
        else:
            side = 1 if dz > 0 else 0
            pair = zs.at[side, :, ys], zr.at[1 - side, 1 - dx, :, yd]
        found.append((*pair, (dx, dy, dz)))
    return found


MESSAGES = 30 + 8 + 26 + 18 + 26 + 11 + 6 + 11 + 4


def kernel(
    sizes, rhs, cond, absb, fx0, fy0, fz0, inv0, diag0, src0, v0, u0,
    e0, mask0, miss0, zs0, zr0, zx0, zq0, edges0,
    e1, fx1, fy1, fz1, inv1, diag1, src1, v1, u1, mask1, miss1, zs1, zr1, zt1, zu1, zv1,
    e2, fx2, fy2, fz2, inv2, diag2, src2, v2, u2, mask2, miss2, own2, cut2, gatc, gats, gatz,
    e3, fx3, fy3, fz3, inv3, diag3, src3, v3, u3, mask3, miss3,
    p01, p12, p23, s32, s21, s10, tmp, send, recv, local, met,
):
    gx, gy, gz = (lax.axis_index(axis) for axis in AXES)
    own0 = (pl.ds(L0.first, L0.nx), pl.ds(0, L0.ny), pl.ds(0, L0.nz))
    loads = [
        pltpu.make_async_copy(source, e0.at[(a,) + own0], local.at[a])
        for a, source in enumerate((cond, absb, rhs))
    ]
    for copy in loads:
        copy.start()

    barrier = pltpu.get_barrier_semaphore()
    faces = [partner(offset, sizes) for offset in NEAR if sum(map(abs, offset)) == 1]

    def greet(semaphore):
        for device in faces:
            pl.semaphore_signal(semaphore, inc=1, device_id=device, device_id_type=MESH)

    greet(barrier)
    started = []

    def post(messages):
        copies = []
        for source, target, offset in messages:
            k = len(started)
            copy = pltpu.make_async_remote_copy(
                src_ref=source,
                dst_ref=target,
                send_sem=send.at[k],
                recv_sem=recv.at[k],
                device_id=partner(offset, sizes),
                device_id_type=MESH,
            )
            copy.start()
            started.append(copy)
            copies.append(copy)
        return copies

    def arrive(copies):
        for copy in copies:
            copy.wait_recv()

    def gather_a(arrays, gat):
        lane = iota((L2.ny, 128), 1)
        group = lax.shift_right_logical(lane, 5)
        for a in arrays:
            low = high = jnp.zeros((L2.ny, 128), F32)
            for q in range(4):
                plane = own2[a, q]
                low = jnp.where(group == q, pltpu.roll(plane, 32 * q, 1) if q else plane, low)
                high = jnp.where(group == q, pltpu.roll(plane, 32 * q - 32, 1) if q > 1 else (plane if q else pltpu.roll(plane, 96, 1)), high)
            cut2[0, a] = low
            cut2[1, a] = high
        if len(arrays) == 2:
            for q in range(4):
                own2[3, q] = jnp.where(lane < 64, own2[0, q], pltpu.roll(own2[1, q], 64, 1))
        whole = 3 if len(arrays) == 2 else arrays[0]
        first = pl.ds(arrays[0], len(arrays))
        mine = pl.ds(L2.nx * gx, L2.nx)
        gat[mine] = own2[whole]
        messages = []
        for dx, dy, dz in GATHER:
            if dz == 0:
                messages.append((own2.at[whole], gat.at[mine], (dx, dy, dz)))
            else:
                side = 1 if dz > 0 else 0
                messages.append((cut2.at[side, first], gatz.at[side, gx, first], (dx, dy, dz)))
        return messages

    def combine(a, gat):
        lane = iota((L2.ny, 128), 1)
        for p in range(16):
            q = p % 4
            far = pltpu.roll(gatz[0, p // 4, a], (64 - 32 * q) % 128, 1) if q != 2 else gatz[0, p // 4, a]
            low = pltpu.roll(gatz[1, p // 4, a], (96 - 32 * q) % 128, 1) if q != 3 else gatz[1, p // 4, a]
            mine = pltpu.roll(gat[p], 64, 1) if a == 1 else gat[p]
            e2[a, L2.first + p, pl.ds(0, 8)] = jnp.where(lane < 64, mine, jnp.where(lane < 96, far, low))

    def gather_b(a, n):
        x = pl.ds(L2.first, 16)
        mine = e2.at[pl.ds(a, n), x, pl.ds(0, 8)]
        messages = [
            (mine, e2.at[pl.ds(a, n), x, pl.ds(row, 8)], (0, dy, 0))
            for dy, row in ((1, 40), (-1, 8), (2, 32), (-2, 16))
        ]
        if a == 0:
            for dy, row, to in ((3, 7, 31), (-3, 0, 24)):
                messages.append(
                    (e2.at[pl.ds(0, 1), x, pl.ds(row, 1)], e2.at[pl.ds(0, 1), x, pl.ds(to, 1)], (0, dy, 0))
                )
        return messages

    messages = fine_messages(L0, (cond, absb, rhs), e0, zs0, zr0, zx0, zq0, edges0)
    pl.semaphore_wait(barrier, 6)
    round_1x = post(messages["x"])
    greet(met.at[0])
    for copy in loads:
        copy.wait()
    round_1 = post(messages["y"])
    pack(L0, 3, 0, e0, zs0)
    pack_edges(L0, zs0, zx0)
    round_1 += post(messages["z"])
    pl.semaphore_wait(met.at[0], 6)
    greet(met.at[1])
    round_1x += post(messages["xy"]) + post(messages["xz"])
    round_1 += post(messages["yz"])
    pl.semaphore_wait(met.at[1], 6)
    round_1x += post(messages["xyz"])
    for lev, mask, miss in ((L0, mask0, miss0), (L1, mask1, miss1), (L2, mask2, miss2), (L3, mask3, miss3)):
        make_mask(lev, sizes, mask, miss)
    p01[...] = pool_matrix(L0, L1)[:256, :128]
    p12[...] = pool_matrix(L1, L2)[:128]
    p23[...] = pool_matrix(L2, L3)
    s32[...] = spread_matrix(L3, L2)
    s21[...] = spread_matrix(L2, L1)
    s10[...] = spread_matrix(L1, L0)
    for p in (0, 1, 18, 19):
        for ref in (e2.at[0], v2, u2):
            ref[p] = jnp.zeros((L2.rows, L2.lanes), F32)
    e2[1, pl.ds(2, 16), pl.ds(24, 8)] = jnp.ones((16, 8, 128), F32)
    e2[2, pl.ds(2, 16), pl.ds(24, 8)] = jnp.zeros((16, 8, 128), F32)
    for p in (0, 9):
        for ref in (e3.at[0], v3, u3):
            ref[p] = jnp.zeros((L3.rows, L3.lanes), F32)

    for a in range(2):

        def stage1(p0, n, a=a):
            for k in range(n):
                q = p0 + k
                p = L0.first + 2 * q
                rows, lanes = pl.ds(0, 32), pl.ds(0, 256)
                stage(tmp, q, e0[a, p, rows, lanes] + e0[a, p + 1, rows, lanes])

        blocks(0, 8, 4, stage1)
        for q, plane in enumerate(pool(tmp, 8, 32, 2, p01)):
            e1[a, L1.first + q, pl.ds(0, 16), pl.ds(0, 128)] = plane
    for a in range(2):
        for q in range(4):
            p = L1.first + 2 * q
            rows, lanes = pl.ds(0, 16), pl.ds(0, 128)
            stage(tmp, 4 * a + q, e1[a, p, rows, lanes] + e1[a, p + 1, rows, lanes])
    for q, plane in enumerate(pool(tmp, 8, 16, 1, p12)):
        own2[q // 4, q % 4] = plane
    round_c2 = post(gather_a((0, 1), gatc))
    pack(L1, 2, 0, e1, zs1)
    round_c1 = post(halo_messages(L1, 0, 2, 6, 6, 3, e1, zs1, zr1))

    base0 = L0.nx * gx - L0.first
    level0 = (fx0, fy0, fz0, inv0)
    arrive(round_1)
    unpack_own(L0, e0, zr0)

    def build0(lo, hi, step=2):
        build(L0, base0, 64, lo, hi, step, e0, mask0, miss0, *level0, diag0, src0, v0, W[0])

    build0(6, 20)
    sweep(7, 19, 2, src0, *level0, v0, u0, W[1])
    arrive(round_1x)
    unpack_edges(L0, e0, zq0)
    build0(3, 6, 3)
    build0(20, 23, 3)
    sweep(4, 7, 3, src0, *level0, v0, u0, W[1])
    sweep(19, 22, 3, src0, *level0, v0, u0, W[1])

    def res0(p):
        return remainder(L0.first + p, src0, fx0, fy0, fz0, diag0, u0)[:32, :256]

    def stage_s1(p0, n):
        for k in range(n):
            q = p0 + k
            stage(tmp, q, res0(2 * q) + res0(2 * q + 1))

    blocks(0, 8, 1, stage_s1)
    for q, plane in enumerate(pool(tmp, 8, 32, 2, p01)):
        for a in (2, 3):
            e1[a, L1.first + q, pl.ds(0, 16), pl.ds(0, 128)] = plane
    pack(L1, 1, 2, e1, zt1)
    round_2 = post(halo_messages(L1, 2, 1, 2, 2, 2, e1, zt1, zu1))

    arrive(round_c2)
    combine(0, gatc)
    combine(1, gatc)
    round_d2 = post(gather_b(0, 2))
    base1 = L1.nx * gx - L1.first
    level1 = (fx1, fy1, fz1, inv1)
    arrive(round_c1)
    unpack(L1, 2, 0, e1, zr1)
    build(L1, base1, 32, 1, 19, 3, e1, mask1, miss1, *level1, diag1, src1, v1, None)

    arrive(round_2)
    unpack(L1, 1, 2, e1, zu1)
    first_sweep(L1, base1, 32, 4, 16, 6, e1.at[2], mask1, inv1, src1, v1, W[0])
    sweep(5, 15, 5, src1, *level1, v1, u1, W[1])

    def res1(p):
        return remainder(L1.first + p, src1, fx1, fy1, fz1, diag1, u1)[:16, :128]

    for q in range(4):
        stage(tmp, q, res1(2 * q) + res1(2 * q + 1))
    for q, plane in enumerate(pool(tmp, 4, 16, 1, p12)):
        own2[2, q] = plane
    round_3 = post(gather_a((2,), gats))
    round_g = post(halo_messages(L1, 3, 1, 5, 6, 3, e1, zt1, zv1))
    round_f = post(messages["far"])
    arrive(round_3)
    combine(2, gats)
    round_4 = post(gather_b(2, 1))

    arrive(round_d2)
    level2 = (fx2, fy2, fz2, inv2)
    level3 = (fx3, fy3, fz3, inv3)
    build(L2, -L2.first, 16, 2, 18, 4, e2, mask2, miss2, *level2, diag2, src2, v2, None)
    for a in range(2):
        for q in range(8):
            stage(tmp, q, e2[a, L2.first + 2 * q] + e2[a, L2.first + 2 * q + 1])
        for q, plane in enumerate(pool(tmp, 8, 48, 1, p23)):
            e3[a, L3.first + q] = plane
    build(L3, -L3.first, 8, 1, 9, 8, e3, mask3, miss3, *level3, diag3, src3, v3, None)

    arrive(round_g)
    unpack(L1, 1, 3, e1, zv1)
    first_sweep(L1, base1, 32, 1, 19, 6, e1.at[3], mask1, inv1, src1, v1, W[0])
    sweep(2, 18, 4, src1, *level1, v1, u1, W[1])
    arrive(round_4)

    first_sweep(L2, -L2.first, 16, 2, 18, 8, e2.at[2], mask2, inv2, src2, v2, W[0])
    sweep(2, 18, 4, src2, *level2, v2, u2, W[1])

    def stage_s3(p0, n):
        for k in range(n):
            q = p0 + k
            pair = [remainder(L2.first + 2 * q + j, src2, fx2, fy2, fz2, diag2, u2) for j in (0, 1)]
            stage(tmp, q, pair[0] + pair[1])

    blocks(0, 8, 2, stage_s3)
    for q, plane in enumerate(pool(tmp, 8, 48, 1, p23)):
        e3[2, L3.first + q] = plane
    first_sweep(L3, -L3.first, 8, 1, 9, 8, e3.at[2], mask3, inv3, src3, v3, W6[0])
    here, there = v3, u3
    for weight in W6[1:]:
        sweep(1, 9, 8, src3, *level3, here, there, weight)
        here, there = there, here

    spread([here[L3.first + q] for q in range(8)], tmp, s32, 24, 0)
    for q in range(8):
        plane = staged(tmp, q, 48, 1)
        for k in (0, 1):
            u2[L2.first + 2 * q + k] += plane
    sweep(2, 18, 4, src2, *level2, u2, v2, W[0])
    sweep(2, 18, 4, src2, *level2, v2, u2, W[1])

    wide = [u2[L2.nx * gx + q] for q in range(8)]
    wide = [jnp.concatenate([plane[:16], plane[40:]], axis=0) for plane in wide]
    spread(wide, tmp, s21, 16, 4)

    def add1(q0, n):
        for j in range(n):
            plane = staged(tmp, q0 + j, 32, 2)
            for k in (0, 1):
                u1[L1.first - 4 + 2 * (q0 + j) + k] += plane

    blocks(0, 8, 2, add1)
    sweep(3, 17, 7, src1, *level1, u1, v1, W[0])
    sweep(4, 16, 6, src1, *level1, v1, u1, W[1])

    arrive(round_f)
    for place in range(4):
        for k in range(4):
            p = (1 if place < 2 else 21) + k
            for a in range(3):
                e0[a, p, pl.ds(40 if place % 2 else 32, 8), pl.ds(0, 256)] = edges0[place, a, k]
    build0(1, 6, 5)
    build0(20, 25, 5)
    sweep(2, 7, 5, src0, *level0, v0, u0, W[1])
    sweep(19, 24, 5, src0, *level0, v0, u0, W[1])

    spread([u1[L1.first - 2 + q] for q in range(12)], tmp, s10, 24, 4)

    def add0(q0, n):
        for j in range(n):
            plane = staged(tmp, q0 + j, 48, 3)
            for k in (0, 1):
                u0[L0.first - 4 + 2 * (q0 + j) + k] += plane

    blocks(0, 12, 2, add0)
    sweep(3, 23, 2, src0, *level0, u0, v0, W[0])
    for copy in started:
        copy.wait_send()


def finish(fx0, fy0, fz0, inv0, diag0, src0, v0, sol_out, res_out, u0, res, done):
    level0 = (fx0, fy0, fz0, inv0)
    copies = []

    def send(source, target):
        copies.append(pltpu.make_async_copy(source, target, done.at[len(copies)]))
        copies[-1].start()

    own = pl.ds(0, 32), pl.ds(0, 256)
    first = L0.first
    sweep(first - 1, first + 1, 2, src0, *level0, v0, u0, W[1])
    for p in range(0, 16, 4):
        lo = p + 1
        sweep(first + lo, first + lo + 4, 4, src0, *level0, v0, u0, W[1])
        send(u0.at[(pl.ds(first + p, 4),) + own], sol_out.at[pl.ds(p, 4)])
    for p in range(0, 16, 4):
        for k in range(p, p + 4):
            res[k] = remainder(first + k, src0, fx0, fy0, fz0, diag0, u0)[:32, :256]
        send(res.at[pl.ds(p, 4)], res_out.at[pl.ds(p, 4)])
    for copy in copies:
        copy.wait()


def solution(mesh):
    sizes = tuple(mesh.shape[axis] for axis in AXES)

    def vmem(*shape):
        return pltpu.VMEM(shape, F32)

    def level(lev, arrays=3):
        return [vmem(arrays, *lev.shape)] + [vmem(*lev.shape)] * 8 + [vmem(lev.rows, lev.lanes)] * 2

    scratch = [
        vmem(3, *L0.shape), vmem(L0.rows, L0.lanes), vmem(L0.rows, L0.lanes), vmem(2, 3, 32, 128), vmem(2, 3, 48, 128), vmem(2, 2, 32, 128), vmem(2, 2, 48, 128), vmem(4, 3, 4, 8, 256),
        *level(L1, 4), vmem(2, 2, 16, 128), vmem(2, 3, 2, 32, 128), vmem(2, 1, 16, 128),
        vmem(2, 3, 1, 32, 128), vmem(2, 3, 1, 32, 128),
        *level(L2), vmem(4, 4, 8, 128), vmem(2, 3, 8, 128), vmem(16, 8, 128), vmem(16, 8, 128), vmem(2, 4, 3, 8, 128),
        *level(L3),
        vmem(256, 128), vmem(128, 128), vmem(128, 128), vmem(128, 128), vmem(128, 256), vmem(256, 384),
        vmem(12, 3, 48, 128),
        pltpu.SemaphoreType.DMA((MESSAGES,)),
        pltpu.SemaphoreType.DMA((MESSAGES,)),
        pltpu.SemaphoreType.DMA((3,)),
        pltpu.SemaphoreType.REGULAR((2,)),
    ]

    def cycle(right_side, conductivity, absorption):
        block = jax.ShapeDtypeStruct((16, 32, 256), F32)
        inner = pl.BlockSpec(memory_space=pltpu.VMEM)
        outer = pl.BlockSpec(memory_space=pltpu.HBM)
        fine = pl.pallas_call(
            functools.partial(kernel, sizes),
            out_shape=(vmem(*L0.shape),) * 8,
            in_specs=[outer] * 3,
            out_specs=(inner,) * 8,
            scratch_shapes=scratch,
            compiler_params=pltpu.CompilerParams(
                collective_id=0, has_side_effects=True, vmem_limit_bytes=49 * 2**20
            ),
        )(right_side, conductivity, absorption)
        return pl.pallas_call(
            finish,
            out_shape=(block, block),
            in_specs=[inner] * 7,
            out_specs=(outer, outer),
            scratch_shapes=[
                vmem(*L0.shape),
                vmem(*block.shape),
                pltpu.SemaphoreType.DMA((8,)),
            ],
            compiler_params=pltpu.CompilerParams(vmem_limit_bytes=12 * 2**20),
        )(*fine[:7])

    placed = P(*AXES)
    return jax.shard_map(
        cycle, mesh=mesh, in_specs=(placed,) * 3, out_specs=(placed, placed), check_vma=False
    )
```

```python
import functools
import math

import jax
import jax.numpy as jnp
from jax import lax
from jax.experimental import pallas as pl
from jax.experimental.pallas import tpu as pltpu
from jax.sharding import PartitionSpec as P

MESH = pl.DeviceIdType.MESH
AXES = ("gx", "gy", "gz")
EIGEN_LOW = 0.25
EIGEN_HIGH = 2.0
F32 = jnp.float32


def chebyshev_weights(count):
    middle = 0.5 * (EIGEN_HIGH + EIGEN_LOW)
    radius = 0.5 * (EIGEN_HIGH - EIGEN_LOW)
    return [
        1.0 / (middle + radius * math.cos(math.pi * (2 * step + 1) / (2 * count)))
        for step in range(count)
    ]


W = chebyshev_weights(2)
W6 = chebyshev_weights(6)


GATHER = [
    (dx, 0, dz) for dx in (1, 3, 2, 0) for dz in (0, 1, -1) if (dx, dz) != (0, 0)
]
NEAR = [
    (dx, dy, dz)
    for dx in (-1, 0, 1)
    for dy in (-1, 0, 1)
    for dz in (-1, 0, 1)
    if (dx, dy, dz) != (0, 0, 0)
]


class Level:
    def __init__(self, scale, own, planes, first, rows, lanes, reach):
        self.scale = scale
        self.nx, self.ny, self.nz = own
        self.planes, self.first = planes, first
        self.rows, self.lanes = rows, lanes
        self.hy, self.hz = reach

    @property
    def shape(self):
        return (self.planes, self.rows, self.lanes)


L0 = Level(1.0, (16, 32, 256), 26, 5, 48, 384, (5, 8))
L1 = Level(0.25, (8, 16, 128), 20, 6, 32, 256, (6, 8))
L2 = Level(0.25**2, (4, 8, 64), 20, 2, 48, 128, (17, 32))
L3 = Level(0.25**3, (2, 4, 32), 10, 1, 24, 128, (8, 16))


def partner(offset, sizes):
    place = []
    for axis, step, size in zip(AXES, offset, sizes):
        index = lax.axis_index(axis)
        place.append(index if step == 0 else lax.rem(index + (step + size), size))
    return tuple(place)


def up(value, axis):
    return pltpu.roll(value, value.shape[axis] - 1, axis)


def down(value, axis):
    return pltpu.roll(value, 1, axis)


def iota(shape, axis):
    return lax.broadcasted_iota(jnp.int32, shape, axis)


def make_mask(lev, sizes, mask_ref, miss_ref):
    shape = (lev.rows, lev.lanes)
    gy, gz = lax.axis_index("gy"), lax.axis_index("gz")
    row, lane = iota(shape, 0), iota(shape, 1)
    y = jnp.where(row < lev.ny + lev.hy, row, row - lev.rows)
    z = jnp.where(lane < lev.nz + lev.hz, lane, lane - lev.lanes)
    yy, zz = y + gy * lev.ny, z + gz * lev.nz
    ymax, zmax = lev.ny * sizes[1], lev.nz * sizes[2]
    good = (y >= -lev.hy) & (z >= -lev.hz) & (yy >= 0) & (yy < ymax) & (zz >= 0) & (zz < zmax)
    mask_ref[...] = jnp.where(good, 1.0, 0.0)
    miss = jnp.where(yy == 0, 1.0, 0.0) + jnp.where(yy == ymax - 1, 1.0, 0.0)
    miss_ref[...] = miss + jnp.where(zz == 0, 1.0, 0.0) + jnp.where(zz == zmax - 1, 1.0, 0.0)


def blocks(lo, hi, step, body):
    full = (hi - lo) // step

    def one(i, carry):
        body(lo + i * step, step)
        return carry

    if full == 1:
        body(lo, step)
    elif full:
        lax.fori_loop(0, full, one, 0)
    if (hi - lo) % step:
        body(lo + full * step, (hi - lo) % step)


def inside(p, base, xmax, mask_ref):
    x = p + base
    return mask_ref[...] > jnp.where((x >= 0) & (x < xmax), 0.5, 2.0)


def build(lev, base, xmax, lo, hi, step, e, mask_ref, miss_ref, fx, fy, fz, inv, diag, src, v, weight):
    scale = lev.scale

    def face(a, b):
        return jnp.where(jnp.minimum(a, b) > 0.0, (0.5 * scale) * (a + b), 0.0)

    def masked(p):
        return jnp.where(inside(p, base, xmax, mask_ref), e[0, p], 0.0)

    fx[lo - 1] = face(masked(lo - 1), masked(lo))

    def body(p0, n):
        cur = masked(p0)
        fxm = fx[p0 - 1]
        for k in range(n):
            p = p0 + k
            x = p + base
            after = masked(p + 1)
            fxp = face(cur, after)
            fx[p] = fxp
            fyp = face(cur, up(cur, 0))
            fy[p] = fyp
            fzp = face(cur, up(cur, 1))
            fz[p] = fzp
            edge = jnp.where(x == 0, 1.0, 0.0) + jnp.where(x == xmax - 1, 1.0, 0.0)
            total = (fxm + fxp) + (fyp + down(fyp, 0)) + (fzp + down(fzp, 1))
            total = total + (scale * cur) * (miss_ref[...] + edge)
            mine = inside(p, base, xmax, mask_ref)
            d = e[1, p] + total
            diag[p] = jnp.where(mine, d, 0.0)
            i = jnp.where(mine, 1.0 / d, 0.0)
            inv[p] = i
            if weight is not None:
                s = jnp.where(mine, e[2, p], 0.0)
                src[p] = s
                v[p] = weight * i * s
            cur, fxm = after, fxp

    blocks(lo, hi, step, body)


def first_sweep(lev, base, xmax, lo, hi, step, source, mask_ref, inv, src, v, weight):
    def body(p0, n):
        for k in range(n):
            p = p0 + k
            s = jnp.where(inside(p, base, xmax, mask_ref), source[p], 0.0)
            src[p] = s
            v[p] = weight * inv[p] * s

    blocks(lo, hi, step, body)


def flow(p, v, fx, fy, fz):
    cur = v[p]
    fyp, fzp = fy[p], fz[p]
    total = fx[p] * v[p + 1] + fx[p - 1] * v[p - 1]
    total = total + (fyp * up(cur, 0) + down(fyp * cur, 0))
    return cur, total + (fzp * up(cur, 1) + down(fzp * cur, 1))


def sweep(lo, hi, step, src, fx, fy, fz, inv, v, out, weight):
    def body(p0, n):
        for k in range(n):
            p = p0 + k
            cur, total = flow(p, v, fx, fy, fz)
            out[p] = (1.0 - weight) * cur + (weight * inv[p]) * (src[p] + total)

    blocks(lo, hi, step, body)


def remainder(p, src, fx, fy, fz, diag, v):
    cur, total = flow(p, v, fx, fy, fz)
    return (src[p] - diag[p] * cur) + total


def pool_matrix(fine, coarse):
    shape = (fine.lanes, coarse.lanes)
    f, c = iota(shape, 0), iota(shape, 1)
    zf = jnp.where(f < fine.nz + fine.hz, f, f - fine.lanes)
    zc = jnp.where(c < coarse.nz + coarse.hz, c, c - coarse.lanes)
    hit = (zf >= 2 * zc) & (zf < 2 * zc + 2) & (zc >= -coarse.hz)
    return jnp.where(hit, 0.125, 0.0)


def spread_matrix(coarse, fine):
    shape = (coarse.lanes, fine.lanes)
    c, f = iota(shape, 0), iota(shape, 1)
    zf = jnp.where(f < fine.nz + fine.hz, f, f - fine.lanes)
    zc = jnp.where(c < coarse.nz + coarse.hz, c, c - coarse.lanes)
    hit = (zf >= 2 * zc) & (zf < 2 * zc + 2) & (zf >= -fine.hz)
    return jnp.where(hit, 1.0, 0.0)


def dot(a, b):
    high = a.astype(jnp.bfloat16)
    low = (a - high.astype(F32)).astype(jnp.bfloat16)
    b = b.astype(jnp.bfloat16)
    return jnp.dot(high, b, preferred_element_type=F32) + jnp.dot(low, b, preferred_element_type=F32)


def stage(tmp, q, plane):
    rows, lanes = plane.shape
    for k in range(lanes // 128):
        tmp[q, k, pl.ds(0, rows)] = plane[:, 128 * k : 128 * (k + 1)]


def pool(tmp, count, rows, tiles, matrix):
    parts = []
    for k in range(tiles):
        lines = []
        for q in range(count):
            even = tmp[q, k, pl.ds(0, rows // 2, stride=2)]
            odd = tmp[q, k, pl.ds(1, rows // 2, stride=2)]
            lines.append(even + odd)
        parts.append(jnp.concatenate(lines, axis=0))
    both = parts[0] if tiles == 1 else jnp.concatenate(parts, axis=1)
    done = dot(both, matrix[...])
    return [done[q * (rows // 2) : (q + 1) * (rows // 2)] for q in range(count)]


def spread(planes, tmp, matrix, rows, wrap):
    size = planes[0].shape[0]
    wide = dot(jnp.concatenate(planes, axis=0), matrix[...])
    for q in range(len(planes)):
        for k in range(wide.shape[1] // 128):
            part = wide[q * size : (q + 1) * size, 128 * k : 128 * (k + 1)]
            for odd in (0, 1):
                tmp[q, k, pl.ds(odd, rows - wrap, stride=2)] = part[: rows - wrap]
                if wrap:
                    tmp[q, k, pl.ds(2 * (rows - wrap) + odd, wrap, stride=2)] = part[size - wrap :]


def staged(tmp, q, rows, tiles):
    parts = [tmp[q, k, pl.ds(0, rows)] for k in range(tiles)]
    return parts[0] if tiles == 1 else jnp.concatenate(parts, axis=1)


def pack(lev, a_count, a_first, e, zs):
    shape = (lev.ny, 128)
    group = lax.shift_right_logical(iota(shape, 1), 3)
    for a in range(a_count):
        low = high = jnp.zeros(shape, F32)
        for x in range(lev.nx):
            p = lev.first + x
            lows = e[a_first + a, p, pl.ds(0, lev.ny), pl.ds(0, 128)]
            highs = e[a_first + a, p, pl.ds(0, lev.ny), pl.ds(lev.nz - 128, 128)]
            if x:
                lows = pltpu.roll(lows, 8 * x, 1)
            if x < 15:
                highs = pltpu.roll(highs, 8 * x + 8, 1)
            low = jnp.where(group == x, lows, low)
            high = jnp.where(group == x, highs, high)
        zs[0, a] = low
        zs[1, a] = high


def pack_edges(lev, zs, zx):
    shape = (lev.ny, 128)
    lane = iota(shape, 1)
    width = 8 * lev.first
    for side in (0, 1):
        for xside in (0, 1):
            total = jnp.zeros(shape, F32)
            for a in range(3):
                shift = width * a - (0 if xside == 0 else 128 - width)
                part = zs[side, a]
                if shift % 128:
                    part = pltpu.roll(part, shift % 128, 1)
                total = jnp.where((lane >= width * a) & (lane < width * (a + 1)), part, total)
            zx[side, xside] = total


def unpack_own(lev, e, zr):
    lane = iota((lev.rows, 128), 1)

    def body(x0, n):
        for k in range(n):
            x = x0 + k
            for a in range(3):
                low = pltpu.roll(zr[0, a], 120 - 8 * x, 1)
                high = pltpu.roll(zr[1, a], lax.rem(128 - 8 * x, 128), 1)
                e[a, lev.first + x, :, pl.ds(lev.nz, 128)] = jnp.where(lane < 64, high, low)

    blocks(0, lev.nx, 4, body)


def unpack_edges(lev, e, zq):
    lane = iota((lev.rows, 128), 1)
    for slot in (0, 1):
        for a in range(3):
            for k in range(lev.first):
                x = a * lev.first + k
                p = k if slot == 0 else lev.first + lev.nx + k
                low = pltpu.roll(zq[0, slot], 120 - 8 * x, 1) if x < 15 else zq[0, slot]
                high = pltpu.roll(zq[1, slot], 128 - 8 * x, 1) if x else zq[1, slot]
                e[a, p, :, pl.ds(lev.nz, 128)] = jnp.where(lane < 64, high, low)


def unpack(lev, a_count, a_first, e, zr):
    lane = iota((lev.rows, 128), 1)
    spans = ((0, 0, lev.first), (1, lev.first, lev.nx), (2, lev.first + lev.nx, lev.first))
    for slot, start, count in spans:
        offset = lev.nx - lev.first if slot == 0 else 0
        for k in range(count):
            x = k + offset
            for a in range(a_count):
                low = pltpu.roll(zr[0, slot, a], 120 - 8 * x, 1)
                high = zr[1, slot, a]
                if x:
                    high = pltpu.roll(high, 128 - 8 * x, 1)
                e[a_first + a, start + k, :, pl.ds(lev.nz, 128)] = jnp.where(lane < 64, high, low)


def fine_messages(lev, inputs, e, zs, zr, zx, zq, edges):
    first, nx, ny, nz, rows, hy = lev.first, lev.nx, lev.ny, lev.nz, lev.rows, lev.hy
    every, lanes = pl.ds(0, 3), pl.ds(0, nz)

    def planes(dx, skip, w):
        if dx == 0:
            return pl.ds(first, nx), pl.ds(first, nx)
        if dx > 0:
            return pl.ds(first + nx - skip - w, w), pl.ds(first - skip - w, w)
        return pl.ds(first + skip, w), pl.ds(first + nx + skip, w)

    def lines(dy, skip=0, w=hy):
        if dy == 0:
            return pl.ds(0, ny), pl.ds(0, ny)
        if dy > 0:
            return pl.ds(ny - skip - w, w), pl.ds(rows - skip - w, w)
        return pl.ds(skip, w), pl.ds(ny + skip, w)

    def flat(dx, dy, arrays, x_part, y_part=(0, hy)):
        xs, xd = planes(dx, *x_part)
        ys, yd = lines(dy, *y_part)
        return e.at[arrays, xs, ys, lanes], e.at[arrays, xd, yd, lanes], (dx, dy, 0)

    found = {key: [] for key in ("x", "y", "z", "xy", "xz", "yz", "xyz", "far", "fars")}
    for dx in (1, -1):
        for a, (whole, w) in enumerate(zip(inputs, (3, 2, 2))):
            xd = planes(dx, 0, w)[1]
            source = whole.at[pl.ds(nx - w if dx > 0 else 0, w)]
            found["x"].append((source, e.at[a, xd, pl.ds(0, ny), lanes], (dx, 0, 0)))
    for dx in (1, -1):
        for dy in (1, -1):
            found["xy"].append(flat(dx, dy, every, (0, 2), (0, 2)))
    for dz in (1, -1):
        side = 1 if dz > 0 else 0
        for dx in (1, -1):
            for dy in (0, 1, -1):
                ys, yd = lines(dy)
                xside = 1 if dx > 0 else 0
                found["xyz" if dy else "xz"].append((zx.at[side, xside, ys], zq.at[1 - side, 1 - xside, yd], (dx, dy, dz)))
    for dy in (1, -1):
        found["y"].append(flat(0, dy, every, (0, nx)))
    for dz in (1, -1):
        side = 1 if dz > 0 else 0
        for dy in (0, 1, -1):
            ys, yd = lines(dy)
            found["yz" if dy else "z"].append((zs.at[side, :, ys], zr.at[1 - side, :, yd], (0, dy, dz)))
    for dx in (1, -1):
        found["far"].append(flat(dx, 0, pl.ds(0, 1), (3, 2)))
        found["far"].append(flat(dx, 0, pl.ds(1, 2), (2, 2)))
        for dy in (1, -1):
            xs, ys = planes(dx, 0, 4)[0], lines(dy, 0, 4)[0]
            low = 1 if dy > 0 else 0
            place = (2 if dx < 0 else 0) + low
            found["fars"].append((e.at[every, xs, ys, lanes], edges.at[place, :, :, pl.ds(4 * low, 4)], (dx, dy, 0)))
    return found


def halo_messages(lev, a_first, a_count, width, hy, axes, e, zs, zr):
    first, nx, ny, rows = lev.first, lev.nx, lev.ny, lev.rows
    arrays, lanes = pl.ds(a_first, a_count), pl.ds(0, lev.nz)

    def planes(dx):
        if dx == 0:
            return pl.ds(first, nx), pl.ds(first, nx)
        if dx > 0:
            return pl.ds(first + nx - width, width), pl.ds(first - width, width)
        return pl.ds(first, width), pl.ds(first + nx, width)

    def lines(dy):
        if dy == 0:
            return pl.ds(0, ny), pl.ds(0, ny)
        if dy > 0:
            return pl.ds(ny - hy, hy), pl.ds(rows - hy, hy)
        return pl.ds(0, hy), pl.ds(ny, hy)

    found = []
    for dx, dy, dz in sorted(NEAR, key=lambda offset: -sum(map(abs, offset))):
        if abs(dx) + abs(dy) + abs(dz) > axes:
            continue
        xs, xd = planes(dx)
        ys, yd = lines(dy)
        if dz == 0:
            pair = e.at[arrays, xs, ys, lanes], e.at[arrays, xd, yd, lanes]
        else:
            side = 1 if dz > 0 else 0
            pair = zs.at[side, :, ys], zr.at[1 - side, 1 - dx, :, yd]
        found.append((*pair, (dx, dy, dz)))
    return found


MESSAGES = 30 + 8 + 26 + 18 + 26 + 11 + 6 + 11 + 4


def kernel(
    sizes, rhs, cond, absb, fx0, fy0, fz0, inv0, diag0, src0, v0, u0,
    e0, mask0, miss0, zs0, zr0, zx0, zq0, edges0,
    e1, fx1, fy1, fz1, inv1, diag1, src1, v1, u1, mask1, miss1, zs1, zr1, zt1, zu1, zv1,
    e2, fx2, fy2, fz2, inv2, diag2, src2, v2, u2, mask2, miss2, own2, cut2, gatc, gats, gatz,
    e3, fx3, fy3, fz3, inv3, diag3, src3, v3, u3, mask3, miss3,
    p01, p12, p23, s32, s21, s10, tmp, send, recv, local, met,
):
    gx, gy, gz = (lax.axis_index(axis) for axis in AXES)
    own0 = (pl.ds(L0.first, L0.nx), pl.ds(0, L0.ny), pl.ds(0, L0.nz))
    loads = [
        pltpu.make_async_copy(source, e0.at[(a,) + own0], local.at[a])
        for a, source in enumerate((cond, absb, rhs))
    ]
    for copy in loads:
        copy.start()

    barrier = pltpu.get_barrier_semaphore()
    faces = [partner(offset, sizes) for offset in NEAR if sum(map(abs, offset)) == 1]

    def greet(semaphore):
        for device in faces:
            pl.semaphore_signal(semaphore, inc=1, device_id=device, device_id_type=MESH)

    greet(barrier)
    started = []

    def post(messages):
        copies = []
        for source, target, offset in messages:
            k = len(started)
            copy = pltpu.make_async_remote_copy(
                src_ref=source,
                dst_ref=target,
                send_sem=send.at[k],
                recv_sem=recv.at[k],
                device_id=partner(offset, sizes),
                device_id_type=MESH,
            )
            copy.start()
            started.append(copy)
            copies.append(copy)
        return copies

    def arrive(copies):
        for copy in copies:
            copy.wait_recv()

    def gather_a(arrays, gat):
        lane = iota((L2.ny, 128), 1)
        group = lax.shift_right_logical(lane, 5)
        for a in arrays:
            low = high = jnp.zeros((L2.ny, 128), F32)
            for q in range(4):
                plane = own2[a, q]
                low = jnp.where(group == q, pltpu.roll(plane, 32 * q, 1) if q else plane, low)
                high = jnp.where(group == q, pltpu.roll(plane, 32 * q - 32, 1) if q > 1 else (plane if q else pltpu.roll(plane, 96, 1)), high)
            cut2[0, a] = low
            cut2[1, a] = high
        if len(arrays) == 2:
            for q in range(4):
                own2[3, q] = jnp.where(lane < 64, own2[0, q], pltpu.roll(own2[1, q], 64, 1))
        whole = 3 if len(arrays) == 2 else arrays[0]
        first = pl.ds(arrays[0], len(arrays))
        mine = pl.ds(L2.nx * gx, L2.nx)
        gat[mine] = own2[whole]
        messages = []
        for dx, dy, dz in GATHER:
            if dz == 0:
                messages.append((own2.at[whole], gat.at[mine], (dx, dy, dz)))
            else:
                side = 1 if dz > 0 else 0
                messages.append((cut2.at[side, first], gatz.at[side, gx, first], (dx, dy, dz)))
        return messages

    def combine(a, gat):
        lane = iota((L2.ny, 128), 1)
        for p in range(16):
            q = p % 4
            far = pltpu.roll(gatz[0, p // 4, a], (64 - 32 * q) % 128, 1) if q != 2 else gatz[0, p // 4, a]
            low = pltpu.roll(gatz[1, p // 4, a], (96 - 32 * q) % 128, 1) if q != 3 else gatz[1, p // 4, a]
            mine = pltpu.roll(gat[p], 64, 1) if a == 1 else gat[p]
            e2[a, L2.first + p, pl.ds(0, 8)] = jnp.where(lane < 64, mine, jnp.where(lane < 96, far, low))

    def gather_b(a, n):
        x = pl.ds(L2.first, 16)
        mine = e2.at[pl.ds(a, n), x, pl.ds(0, 8)]
        messages = [
            (mine, e2.at[pl.ds(a, n), x, pl.ds(row, 8)], (0, dy, 0))
            for dy, row in ((1, 40), (-1, 8), (2, 32), (-2, 16))
        ]
        if a == 0:
            for dy, row, to in ((3, 7, 31), (-3, 0, 24)):
                messages.append(
                    (e2.at[pl.ds(0, 1), x, pl.ds(row, 1)], e2.at[pl.ds(0, 1), x, pl.ds(to, 1)], (0, dy, 0))
                )
        return messages

    messages = fine_messages(L0, (cond, absb, rhs), e0, zs0, zr0, zx0, zq0, edges0)
    pl.semaphore_wait(barrier, 6)
    round_1x = post(messages["x"])
    greet(met.at[0])
    for copy in loads:
        copy.wait()
    round_1 = post(messages["y"])
    pack(L0, 3, 0, e0, zs0)
    pack_edges(L0, zs0, zx0)
    round_1 += post(messages["z"])
    pl.semaphore_wait(met.at[0], 6)
    greet(met.at[1])
    round_1x += post(messages["xy"]) + post(messages["xz"])
    round_1 += post(messages["yz"])
    pl.semaphore_wait(met.at[1], 6)
    round_1x += post(messages["xyz"])
    for lev, mask, miss in ((L0, mask0, miss0), (L1, mask1, miss1), (L2, mask2, miss2), (L3, mask3, miss3)):
        make_mask(lev, sizes, mask, miss)
    p01[...] = pool_matrix(L0, L1)[:256, :128]
    p12[...] = pool_matrix(L1, L2)[:128]
    p23[...] = pool_matrix(L2, L3)
    s32[...] = spread_matrix(L3, L2)
    s21[...] = spread_matrix(L2, L1)
    s10[...] = spread_matrix(L1, L0)
    for p in (0, 1, 18, 19):
        for ref in (e2.at[0], v2, u2):
            ref[p] = jnp.zeros((L2.rows, L2.lanes), F32)
    e2[1, pl.ds(2, 16), pl.ds(24, 8)] = jnp.ones((16, 8, 128), F32)
    e2[2, pl.ds(2, 16), pl.ds(24, 8)] = jnp.zeros((16, 8, 128), F32)
    for p in (0, 9):
        for ref in (e3.at[0], v3, u3):
            ref[p] = jnp.zeros((L3.rows, L3.lanes), F32)

    for a in range(2):

        def stage1(p0, n, a=a):
            for k in range(n):
                q = p0 + k
                p = L0.first + 2 * q
                rows, lanes = pl.ds(0, 32), pl.ds(0, 256)
                stage(tmp, q, e0[a, p, rows, lanes] + e0[a, p + 1, rows, lanes])

        blocks(0, 8, 4, stage1)
        for q, plane in enumerate(pool(tmp, 8, 32, 2, p01)):
            e1[a, L1.first + q, pl.ds(0, 16), pl.ds(0, 128)] = plane
    for a in range(2):
        for q in range(4):
            p = L1.first + 2 * q
            rows, lanes = pl.ds(0, 16), pl.ds(0, 128)
            stage(tmp, 4 * a + q, e1[a, p, rows, lanes] + e1[a, p + 1, rows, lanes])
    for q, plane in enumerate(pool(tmp, 8, 16, 1, p12)):
        own2[q // 4, q % 4] = plane
    round_c2 = post(gather_a((0, 1), gatc))
    pack(L1, 2, 0, e1, zs1)
    round_c1 = post(halo_messages(L1, 0, 2, 6, 6, 3, e1, zs1, zr1))

    base0 = L0.nx * gx - L0.first
    level0 = (fx0, fy0, fz0, inv0)
    arrive(round_1)
    unpack_own(L0, e0, zr0)

    def build0(lo, hi, step=2):
        build(L0, base0, 64, lo, hi, step, e0, mask0, miss0, *level0, diag0, src0, v0, W[0])

    build0(6, 20)
    sweep(7, 19, 2, src0, *level0, v0, u0, W[1])
    arrive(round_1x)
    unpack_edges(L0, e0, zq0)
    build0(3, 6, 3)
    build0(20, 23, 3)
    sweep(4, 7, 3, src0, *level0, v0, u0, W[1])
    sweep(19, 22, 3, src0, *level0, v0, u0, W[1])

    def res0(p):
        return remainder(L0.first + p, src0, fx0, fy0, fz0, diag0, u0)[:32, :256]

    def stage_s1(p0, n):
        for k in range(n):
            q = p0 + k
            stage(tmp, q, res0(2 * q) + res0(2 * q + 1))

    blocks(0, 8, 2, stage_s1)
    for q, plane in enumerate(pool(tmp, 8, 32, 2, p01)):
        for a in (2, 3):
            e1[a, L1.first + q, pl.ds(0, 16), pl.ds(0, 128)] = plane
    pack(L1, 1, 2, e1, zt1)
    round_2 = post(halo_messages(L1, 2, 1, 2, 2, 2, e1, zt1, zu1))
    round_f = post(messages["far"])

    arrive(round_c2)
    combine(0, gatc)
    combine(1, gatc)
    round_d2 = post(gather_b(0, 2))
    base1 = L1.nx * gx - L1.first
    level1 = (fx1, fy1, fz1, inv1)
    arrive(round_c1)
    unpack(L1, 2, 0, e1, zr1)
    build(L1, base1, 32, 1, 19, 3, e1, mask1, miss1, *level1, diag1, src1, v1, None)

    arrive(round_2)
    unpack(L1, 1, 2, e1, zu1)
    first_sweep(L1, base1, 32, 4, 16, 6, e1.at[2], mask1, inv1, src1, v1, W[0])
    sweep(5, 15, 5, src1, *level1, v1, u1, W[1])

    def res1(p):
        return remainder(L1.first + p, src1, fx1, fy1, fz1, diag1, u1)[:16, :128]

    for q in range(4):
        stage(tmp, q, res1(2 * q) + res1(2 * q + 1))
    for q, plane in enumerate(pool(tmp, 4, 16, 1, p12)):
        own2[2, q] = plane
    round_3 = post(gather_a((2,), gats))
    round_g = post(halo_messages(L1, 3, 1, 5, 6, 3, e1, zt1, zv1))
    round_f += post(messages["fars"])
    arrive(round_3)
    combine(2, gats)
    round_4 = post(gather_b(2, 1))

    arrive(round_d2)
    level2 = (fx2, fy2, fz2, inv2)
    level3 = (fx3, fy3, fz3, inv3)
    build(L2, -L2.first, 16, 2, 18, 4, e2, mask2, miss2, *level2, diag2, src2, v2, None)
    for a in range(2):
        for q in range(8):
            stage(tmp, q, e2[a, L2.first + 2 * q] + e2[a, L2.first + 2 * q + 1])
        for q, plane in enumerate(pool(tmp, 8, 48, 1, p23)):
            e3[a, L3.first + q] = plane
    build(L3, -L3.first, 8, 1, 9, 8, e3, mask3, miss3, *level3, diag3, src3, v3, None)

    arrive(round_g)
    unpack(L1, 1, 3, e1, zv1)
    first_sweep(L1, base1, 32, 1, 19, 6, e1.at[3], mask1, inv1, src1, v1, W[0])
    sweep(2, 18, 4, src1, *level1, v1, u1, W[1])
    arrive(round_f)
    for place in range(4):
        for k in range(4):
            p = (1 if place < 2 else 21) + k
            for a in range(3):
                e0[a, p, pl.ds(40 if place % 2 else 32, 8), pl.ds(0, 256)] = edges0[place, a, k]
    build0(1, 6, 5)
    build0(20, 25, 5)
    sweep(2, 7, 5, src0, *level0, v0, u0, W[1])
    sweep(19, 24, 5, src0, *level0, v0, u0, W[1])

    arrive(round_4)

    first_sweep(L2, -L2.first, 16, 2, 18, 8, e2.at[2], mask2, inv2, src2, v2, W[0])
    sweep(2, 18, 4, src2, *level2, v2, u2, W[1])

    def stage_s3(p0, n):
        for k in range(n):
            q = p0 + k
            pair = [remainder(L2.first + 2 * q + j, src2, fx2, fy2, fz2, diag2, u2) for j in (0, 1)]
            stage(tmp, q, pair[0] + pair[1])

    blocks(0, 8, 2, stage_s3)
    for q, plane in enumerate(pool(tmp, 8, 48, 1, p23)):
        e3[2, L3.first + q] = plane
    first_sweep(L3, -L3.first, 8, 1, 9, 8, e3.at[2], mask3, inv3, src3, v3, W6[0])
    here, there = v3, u3
    for weight in W6[1:]:
        sweep(1, 9, 8, src3, *level3, here, there, weight)
        here, there = there, here

    spread([here[L3.first + q] for q in range(8)], tmp, s32, 24, 0)
    for q in range(8):
        plane = staged(tmp, q, 48, 1)
        for k in (0, 1):
            u2[L2.first + 2 * q + k] += plane
    sweep(2, 18, 4, src2, *level2, u2, v2, W[0])
    sweep(2, 18, 4, src2, *level2, v2, u2, W[1])

    wide = [u2[L2.nx * gx + q] for q in range(8)]
    wide = [jnp.concatenate([plane[:16], plane[40:]], axis=0) for plane in wide]
    spread(wide, tmp, s21, 16, 4)

    def add1(q0, n):
        for j in range(n):
            plane = staged(tmp, q0 + j, 32, 2)
            for k in (0, 1):
                u1[L1.first - 4 + 2 * (q0 + j) + k] += plane

    blocks(0, 8, 2, add1)
    sweep(3, 17, 7, src1, *level1, u1, v1, W[0])
    sweep(4, 16, 6, src1, *level1, v1, u1, W[1])

    spread([u1[L1.first - 2 + q] for q in range(12)], tmp, s10, 24, 4)

    def add0(q0, n):
        for j in range(n):
            plane = staged(tmp, q0 + j, 48, 3)
            for k in (0, 1):
                u0[L0.first - 4 + 2 * (q0 + j) + k] += plane

    blocks(0, 12, 2, add0)
    sweep(3, 23, 2, src0, *level0, u0, v0, W[0])
    for copy in started:
        copy.wait_send()


def finish(fx0, fy0, fz0, inv0, diag0, src0, v0, sol_out, res_out, u0, res, done):
    level0 = (fx0, fy0, fz0, inv0)
    copies = []

    def send(source, target):
        copies.append(pltpu.make_async_copy(source, target, done.at[len(copies)]))
        copies[-1].start()

    own = pl.ds(0, 32), pl.ds(0, 256)
    first = L0.first
    sweep(first - 1, first + 1, 2, src0, *level0, v0, u0, W[1])
    for p in range(0, 16, 4):
        lo = p + 1
        sweep(first + lo, first + lo + 4, 4, src0, *level0, v0, u0, W[1])
        send(u0.at[(pl.ds(first + p, 4),) + own], sol_out.at[pl.ds(p, 4)])
    for p in range(0, 16, 4):
        for k in range(p, p + 4):
            res[k] = remainder(first + k, src0, fx0, fy0, fz0, diag0, u0)[:32, :256]
        send(res.at[pl.ds(p, 4)], res_out.at[pl.ds(p, 4)])
    for copy in copies:
        copy.wait()


def solution(mesh):
    sizes = tuple(mesh.shape[axis] for axis in AXES)

    def vmem(*shape):
        return pltpu.VMEM(shape, F32)

    def level(lev, arrays=3):
        return [vmem(arrays, *lev.shape)] + [vmem(*lev.shape)] * 8 + [vmem(lev.rows, lev.lanes)] * 2

    scratch = [
        vmem(3, *L0.shape), vmem(L0.rows, L0.lanes), vmem(L0.rows, L0.lanes), vmem(2, 3, 32, 128), vmem(2, 3, 48, 128), vmem(2, 2, 32, 128), vmem(2, 2, 48, 128), vmem(4, 3, 4, 8, 256),
        *level(L1, 4), vmem(2, 2, 16, 128), vmem(2, 3, 2, 32, 128), vmem(2, 1, 16, 128),
        vmem(2, 3, 1, 32, 128), vmem(2, 3, 1, 32, 128),
        *level(L2), vmem(4, 4, 8, 128), vmem(2, 3, 8, 128), vmem(16, 8, 128), vmem(16, 8, 128), vmem(2, 4, 3, 8, 128),
        *level(L3),
        vmem(256, 128), vmem(128, 128), vmem(128, 128), vmem(128, 128), vmem(128, 256), vmem(256, 384),
        vmem(12, 3, 48, 128),
        pltpu.SemaphoreType.DMA((MESSAGES,)),
        pltpu.SemaphoreType.DMA((MESSAGES,)),
        pltpu.SemaphoreType.DMA((3,)),
        pltpu.SemaphoreType.REGULAR((2,)),
    ]

    def cycle(right_side, conductivity, absorption):
        block = jax.ShapeDtypeStruct((16, 32, 256), F32)
        inner = pl.BlockSpec(memory_space=pltpu.VMEM)
        outer = pl.BlockSpec(memory_space=pltpu.HBM)
        fine = pl.pallas_call(
            functools.partial(kernel, sizes),
            out_shape=(vmem(*L0.shape),) * 8,
            in_specs=[outer] * 3,
            out_specs=(inner,) * 8,
            scratch_shapes=scratch,
            compiler_params=pltpu.CompilerParams(
                collective_id=0, has_side_effects=True, vmem_limit_bytes=49 * 2**20
            ),
        )(right_side, conductivity, absorption)
        return pl.pallas_call(
            finish,
            out_shape=(block, block),
            in_specs=[inner] * 7,
            out_specs=(outer, outer),
            scratch_shapes=[
                vmem(*L0.shape),
                vmem(*block.shape),
                pltpu.SemaphoreType.DMA((8,)),
            ],
            compiler_params=pltpu.CompilerParams(vmem_limit_bytes=12 * 2**20),
        )(*fine[:7])

    placed = P(*AXES)
    return jax.shard_map(
        cycle, mesh=mesh, in_specs=(placed,) * 3, out_specs=(placed, placed), check_vma=False
    )
```
